256 devices in a mesh: section: 16 (over y, z_hi), peer: 16 (over x, z_lo, core).
Axes of the slice: x: 4, y: 4, z: 8 (z_hi: 4, z_lo: 2; z = z_hi * 2 + z_lo), core: 2. Of those that a mesh axis runs over, the one named last changes fastest.
Arguments:
- acts_fwd: bfloat16 [16, 4096, 2560], P('section', 'peer'), may hold values from -30 to 30
- acts_bwd: bfloat16 [16, 4096, 2560], P('section', 'peer'), may hold values from -30 to 30
- cot_bwd: bfloat16 [16, 4096, 2560], P('section', 'peer'), may hold values from -6 to 6
- gain: float32 [16, 2560], P('section'), may hold values from 0.1 to 1.9
- proj: bfloat16 [16, 2560, 2560], P('section', 'peer'), may hold values from -0.125 to 0.125
- fwd_route: int32 [16, 256, 1], P('section', 'peer'), may hold values from 0 to 15; in each aligned block of 16 rows (0 to 15, 16 to 31, ..., all dimensions but the last counted through in order) no two rows name the same one
- bwd_route: int32 [16, 256, 1], P('section', 'peer'), may hold values from 0 to 15; in each aligned block of 16 rows (0 to 15, 16 to 31, ..., all dimensions but the last counted through in order) no two rows name the same one
- straggler: int32 [16, 16], P('section'), may hold values from 0 to 1, as said below
Outputs:
- next_acts: bfloat16 [16, 4096, 2560], P('section', 'peer')
- back_grads: bfloat16 [16, 4096, 2560], P('section', 'peer')
- weight_gradient_mean: float32 [16, 2560, 2560], P('section', 'peer')
The draws below stay inside these ranges and needn't reach their ends.
Inputs may be any that keep to these rules, and one draw needn't show every extreme that they name: `fwd_route`: among the 16 blocks of one peer of one section, every peer index appears exactly 1 times. `bwd_route`: among the 16 blocks of one peer of one section, every peer index appears exactly 1 times. `straggler`: in every section at least one peer is not excluded.
All inputs are finite; a program needn't handle non-finite values.
Results may differ from the reference program's by a relative error of at most 0.019.
Values may be sent and summed in bfloat16 or wider, within the bound.
A program may use at most 192 MiB of HBM per device.

```python
import math
import jax
import jax.numpy as jnp
import numpy as np
from jax import lax

C = 2560
TOK_DEV = 256
BLK = 16
NBLK = 16
CAP = 1
ROWS = 4096
N_SECTION = 16
N_PEER = 16


def spread_field(base_field, key_rows, key_cols):
    row_scale = jnp.exp(jax.random.uniform(key_rows, (N_SECTION, ROWS, 1), jnp.float32, math.log(0.3), math.log(3.0)))
    col_scale = jnp.exp(jax.random.uniform(key_cols, (1, 1, C), jnp.float32, math.log(0.5), math.log(2.0)))
    return (base_field * row_scale * col_scale).astype(jnp.bfloat16)


def draw_acts_fwd(key, part):
    key = jax.random.fold_in(key, 11)
    subkeys = jax.random.split(key, 3)
    base_field = jnp.clip(jax.random.normal(subkeys[0], (N_SECTION, ROWS, C), jnp.float32), -5.0, 5.0)
    return spread_field(base_field, subkeys[1], subkeys[2])


def draw_acts_bwd(key, part):
    key = jax.random.fold_in(key, 12)
    subkeys = jax.random.split(key, 3)
    base_field = jnp.clip(jax.random.normal(subkeys[0], (N_SECTION, ROWS, C), jnp.float32), -5.0, 5.0)
    return spread_field(base_field, subkeys[1], subkeys[2])


def draw_straggler(key, part):
    key = jax.random.fold_in(key, 5)
    key_mask, key_retained = jax.random.split(key, 2)
    excluded = (jax.random.randint(key_mask, (N_SECTION, N_PEER), 0, 4) == 0).astype(jnp.int32)
    remaining_peer = jax.random.randint(key_retained, (N_SECTION, 1), 0, N_PEER)
    single_kept_peer = (jnp.arange(N_PEER, dtype=jnp.int32)[None, :] == remaining_peer).astype(jnp.int32)
    return excluded * (1 - single_kept_peer)


def shard_levels(own_key, extent, cuts, smallest, top_value):
    factor_of = 1.0
    for dim, blocks in cuts:
        heights = jax.random.uniform(jax.random.fold_in(jax.random.fold_in(own_key, 6), dim), (blocks,), jnp.float32, smallest / len(cuts), top_value / len(cuts))
        factor_of = factor_of * jnp.repeat(jnp.exp(heights), extent[dim] // blocks).reshape((-1,) + (1,) * (len(extent) - 1 - dim))
    return factor_of


def routed_block(stream_key, own, number, rows, number_of, top, bound, skew):
    ranking = jax.random.permutation(stream_key, number_of)
    crowded, usual = portions_of(number_of, rows * top, bound, skew, True), portions_of(number_of, rows * top, bound, skew, False)
    places = jnp.arange(number_of)

    def named(tallies, turn):
        used = int((tallies > 0).sum())
        fixed = max(1, used // 4)
        moved = fixed + (places - fixed + turn * (used - fixed)) % max(1, number_of - fixed)
        return jnp.zeros((number_of,), jnp.int32).at[ranking[jnp.where(places < fixed, places, moved)]].set(jnp.asarray(tallies, jnp.int32))

    tallies = jnp.where(number % 4 == 0, named(crowded, number // 4), named(usual, number - number // 4 - 1))
    mixed = jax.random.permutation(jax.random.fold_in(own, 3), number_of)
    giver, receiver = mixed[0:number_of // 2 * 2:2], mixed[1:number_of // 2 * 2:2]
    room = jnp.minimum(tallies[giver] - 1, bound - tallies[receiver]) // 2
    room = jnp.where((giver == ranking[0]) | (receiver == ranking[0]) | (tallies[receiver] == 0), 0, jnp.maximum(room, 0))
    moved = jax.random.randint(jax.random.fold_in(own, 4), (number_of // 2,), 0, 1 << 20) % (room + 1)
    tallies = tallies.at[giver].add(-moved).at[receiver].add(moved)
    members = jnp.searchsorted(jnp.cumsum(tallies), jnp.arange(rows * top), side="right").astype(jnp.int32)
    table = members.reshape(top, rows).T
    table = table[jax.random.permutation(jax.random.fold_in(own, 1), rows)]
    turn = jax.random.randint(jax.random.fold_in(own, 2), (rows, 1), 0, top)
    return jnp.take_along_axis(table, (jnp.arange(top)[None, :] + turn) % top, axis=1)


def portions_of(count, total, limit, lean, full):
    portions = [(1 << 20) // math.isqrt(grade ** lean) + 1 for grade in range(1, count + 1)]
    largest = limit if full else min(limit, max(-(-total // count), total * portions[0] // sum(portions)))
    least = 1 if total - largest >= count - 1 else 0
    counts, rest = [largest] + [least] * (count - 1), total - largest - least * (count - 1)
    while rest > 0:
        candidates = [i for i in range(1, count) if counts[i] < largest] or [i for i in range(1, count) if counts[i] < limit]
        mass, budget = sum([portions[i] for i in candidates]), rest
        for i in candidates:
            extra = min(limit - counts[i], max(1, budget * portions[i] // mass), rest)
            counts[i] = counts[i] + extra
            rest = rest - extra
    return np.array(counts)


def normal_values(rng, shape, width, limit, shards=(), kind=jnp.bfloat16):
    array = width * jax.random.normal(rng, shape, jnp.float32)
    if shards:
        array = array * shard_levels(rng, shape, shards, -0.22, 0.18)
    return jnp.clip(array, -limit, limit).astype(kind)


def setup_inputs(seed: int = 0) -> dict:
    keys = jax.random.split(jax.random.key(seed), 9)
    acts_fwd = draw_acts_fwd(jax.random.fold_in(keys[8], 71), 0)
    acts_bwd = draw_acts_bwd(jax.random.fold_in(keys[8], 71), 0)
    cot_bwd = normal_values(keys[2], (N_SECTION, ROWS, C), 1.0, 6.0, ((0, 16), (1, 16)))
    gain = jnp.clip(1.0 + 0.18 * jax.random.normal(keys[3], (N_SECTION, C), jnp.float32), 0.1, 1.9)
    proj = normal_values(keys[4], (N_SECTION, C, C), C ** -0.5, 0.125, ((0, 16), (1, 16)))
    fwd_route_keys = jax.random.split(jax.random.fold_in(keys[5], 1), N_SECTION * (NBLK * N_PEER) // NBLK)
    fwd_route_turns = jax.random.permutation(jax.random.fold_in(keys[5], 3), N_SECTION * (NBLK * N_PEER) // NBLK)
    fwd_route = jax.vmap(lambda own, number: routed_block(jax.random.fold_in(keys[5], 2), own, number, NBLK, N_PEER, 1, CAP, 0))(fwd_route_keys, fwd_route_turns).reshape((N_SECTION, NBLK * N_PEER, 1))
    bwd_route_keys = jax.random.split(jax.random.fold_in(keys[6], 1), N_SECTION * (NBLK * N_PEER) // NBLK)
    bwd_route_turns = jax.random.permutation(jax.random.fold_in(keys[6], 3), N_SECTION * (NBLK * N_PEER) // NBLK)
    bwd_route = jax.vmap(lambda own, number: routed_block(jax.random.fold_in(keys[6], 2), own, number, NBLK, N_PEER, 1, CAP, 0))(bwd_route_keys, bwd_route_turns).reshape((N_SECTION, NBLK * N_PEER, 1))
    straggler = draw_straggler(jax.random.fold_in(keys[8], 71), 0)
    return dict(acts_fwd=acts_fwd, acts_bwd=acts_bwd, cot_bwd=cot_bwd, gain=gain, proj=proj, fwd_route=fwd_route, bwd_route=bwd_route, straggler=straggler)


epsilon = 1e-05

def normalize(values, gain_row):
    wide_vals = values.astype(jnp.float32)
    scale_row = lax.rsqrt(lax.optimization_barrier(jnp.mean(wide_vals * wide_vals, axis=-1, keepdims=True)) + epsilon)
    return (wide_vals, scale_row, (wide_vals * scale_row * gain_row).astype(jnp.bfloat16))

def route_section(section_rows, route_table):
    dest_peer = route_table.reshape(N_PEER, NBLK)
    same_dest = dest_peer[:, :, None] == dest_peer[:, None, :]
    earlier = jnp.arange(NBLK)[None, :, None] > jnp.arange(NBLK)[None, None, :]
    slot_rank = lax.optimization_barrier(jnp.sum((same_dest & earlier).astype(jnp.int32), axis=2))
    sender = jnp.arange(N_PEER, dtype=jnp.int32)[:, None]
    target = dest_peer * (N_PEER * CAP) + sender * CAP + slot_rank
    source_order = jnp.argsort(target.reshape(-1))
    flat_blocks = section_rows.reshape(N_PEER * NBLK, BLK * C)
    return jnp.take(flat_blocks, source_order, axis=0).reshape(ROWS, C)

def section_step(inputs):
    acts_a, acts_b, cot_b, gain_row, weight, keep_row = inputs
    wide_a, scale_a, normed_a = normalize(acts_a, gain_row)
    wide_b, scale_b, normed_b = normalize(acts_b, gain_row)
    weight_wide = weight.astype(jnp.float32)
    hidden = jnp.dot(normed_a.astype(jnp.float32), weight_wide, preferred_element_type=jnp.float32)
    out_a = (wide_a + hidden).astype(jnp.bfloat16)
    cot_wide = cot_b.astype(jnp.float32)
    grad_normed = jnp.dot(cot_wide, weight_wide.T, preferred_element_type=jnp.float32)
    scaled = gain_row * grad_normed
    inner = lax.optimization_barrier(jnp.mean(wide_b * scaled, axis=-1, keepdims=True))
    grad_in = (cot_wide + scale_b * scaled - wide_b * scale_b * scale_b * scale_b * inner).astype(jnp.bfloat16)

    def add_peer(running, peer_id):
        first_row = (peer_id * TOK_DEV).astype(jnp.int32)
        normed_p = lax.dynamic_slice_in_dim(normed_b, first_row, TOK_DEV, 0).astype(jnp.float32)
        cot_p = lax.dynamic_slice_in_dim(cot_b, first_row, TOK_DEV, 0).astype(jnp.float32)
        partial_value = jnp.dot(normed_p.T, cot_p, preferred_element_type=jnp.float32).astype(jnp.bfloat16)
        partial_value = lax.optimization_barrier(partial_value).astype(jnp.float32)
        return (running + keep_row[peer_id] * partial_value, None)
    running, ignored = lax.scan(add_peer, jnp.zeros((C, C), jnp.float32), jnp.arange(N_PEER, dtype=jnp.int32))
    weight_gradient_mean = running / jnp.sum(keep_row)
    return (out_a, grad_in, weight_gradient_mean)

def route_pair(inputs):
    section_rows, route_table = inputs
    return route_section(section_rows, route_table)

def reference(acts_fwd, acts_bwd, cot_bwd, gain, proj, fwd_route, bwd_route, straggler):
    keep_table = 1.0 - straggler.astype(jnp.float32)
    out_a, grad_in, weight_gradient_mean = lax.map(section_step, (acts_fwd, acts_bwd, cot_bwd, gain, proj, keep_table))
    routed_up = lax.map(route_pair, (out_a, fwd_route[:, :, 0]))
    routed_down = lax.map(route_pair, (grad_in, bwd_route[:, :, 0]))
    empty_section = jnp.zeros_like(routed_up[:1])
    next_acts = jnp.concatenate([empty_section, routed_up[:-1]], axis=0)
    back_grads = jnp.concatenate([routed_down[1:], empty_section], axis=0)
    return (next_acts, back_grads, weight_gradient_mean)
```

```python
import jax
import jax.numpy as jnp
from jax import lax
from jax.experimental import pallas as pl
from jax.experimental.pallas import tpu as pltpu
from jax.sharding import PartitionSpec as P

MESH = pl.DeviceIdType.MESH
F32 = jnp.float32
BF16 = jnp.bfloat16
EPS = 1e-05

SECTIONS = 16
PEERS = 16
C = 2560
TOK = 256
BLK = 16
SH = C // PEERS
HALF = SH // 2
GRP = 4 * SH
TILE = 512


def dot(a, b, dims):
    return lax.dot_general(a, b, (dims, ((), ())), preferred_element_type=F32)


def kernel(
    acts_f, acts_b, cot, gain, proj, froute, broute, strag,
    next_o, back_o, dw_o,
    wg, af, ab, aperm, bperm, cperm, na, nb, nbt, nbq, cotq, hacc, gn, ostage, gstage,
    psend, rs_half, rs_full,
    loc_sem, ag_ss, ag_rs, sib_ss, sib_rs, ex_ss, ex_rs, nb_ss, nb_rs, red_ss, red_rs, a2a_ss, a2a_rs,
):
    s = lax.axis_index("section")
    q = lax.axis_index("peer")
    x = lax.div(q, 4)
    quad = lax.rem(q, 4)
    z = lax.div(quad, 2)
    c = lax.rem(q, 2)
    xr = lax.rem(x + 1, 4)
    xl = lax.rem(x + 3, 4)
    x2 = lax.rem(x + 2, 4)
    up = lax.rem(s + 1, SECTIONS)
    down = lax.rem(s + SECTIONS - 1, SECTIONS)

    def peer(px, pz, pc):
        return px * 4 + pz * 2 + pc

    right = (s, peer(xr, z, c))
    left = (s, peer(xl, z, c))
    zpart = (s, peer(x, 1 - z, c))
    sib = (s, peer(x, z, 1 - c))
    diag = (s, peer(x, 1 - z, 1 - c))

    bar = pltpu.get_barrier_semaphore()
    for dev in (right, left, zpart, sib, diag):
        pl.semaphore_signal(bar, inc=1, device_id=dev, device_id_type=MESH)

    def greet(i, carry):
        pl.semaphore_signal(bar, inc=1, device_id=(up, i), device_id_type=MESH)
        pl.semaphore_signal(bar, inc=1, device_id=(down, i), device_id_type=MESH)
        return carry

    lax.fori_loop(0, PEERS, greet, 0)
    pl.semaphore_wait(bar, 5 + 2 * PEERS)

    def remote(src, dst, ss, rs, dev):
        return pltpu.make_async_remote_copy(
            src_ref=src, dst_ref=dst, send_sem=ss, recv_sem=rs, device_id=dev, device_id_type=MESH
        )

    def rows(px, pz, lo=0, n=SH, pc=c):
        return wg.at[pl.ds(pl.multiple_of(peer(px, pz, pc) * SH + lo, 16), n)]

    sent = []

    def send(src, dst, ss, rs, dev):
        cp = remote(src, dst, ss, rs, dev)
        cp.start()
        sent.append(cp)

    def ag_send(src, region, k_send, k_recv, dev):
        send(src, region, ag_ss.at[k_send], ag_rs.at[k_recv], dev)

    def ag_wait(region, k_recv):
        remote(region, region, ag_ss.at[0], ag_rs.at[k_recv], zpart).wait_recv()

    def sib_send(src, region, k):
        send(src, region, sib_ss.at[k], sib_rs.at[k], sib)

    def sib_wait(px, pz, k, lo=0, n=SH):
        region = rows(px, pz, lo, n, 1 - c)
        remote(region, region, sib_ss.at[k], sib_rs.at[k], sib).wait_recv()

    ag_send(proj, rows(x, z), 0, 0, zpart)
    ag_send(proj, rows(x, z), 1, 1, right)
    ag_send(proj, rows(x, z), 2, 5, left)
    sib_send(proj, rows(x, z), 0)
    own_slot = pl.ds(pl.multiple_of(quad * TOK, TOK), TOK)
    loads = [
        pltpu.make_async_copy(acts_b, ab, loc_sem.at[0]),
        pltpu.make_async_copy(acts_f, af, loc_sem.at[1]),
        pltpu.make_async_copy(cot, cotq.at[own_slot], loc_sem.at[2]),
        pltpu.make_async_copy(proj, rows(x, z), loc_sem.at[3]),
    ]
    for cp in loads:
        cp.start()
    send(cot, cotq.at[own_slot], ex_ss.at[0], ex_rs.at[0], sib)

    count = jnp.float32(0)
    for i in range(PEERS):
        count = count + (1 - strag[0, i]).astype(F32)
    keep = (1 - strag[0, q]).astype(F32)

    loads[0].wait()

    def norm_b(i, carry):
        r = pl.ds(pl.multiple_of(i * 16, 16), 16)
        wide = ab[r].astype(F32)
        rstd = lax.rsqrt(jnp.mean(wide * wide, axis=-1, keepdims=True) + EPS)
        nb[r] = (wide * rstd * gain[...] * keep).astype(BF16)
        return carry

    lax.fori_loop(0, TOK // 16, norm_b, 0)

    def turn(i, carry):
        cols = pl.ds(pl.multiple_of(i * GRP, GRP), GRP)
        t = nb[:, cols].T
        for k in range(4):
            nbt[k, pl.ds(pl.multiple_of(i * SH, SH), SH)] = t[k * SH:(k + 1) * SH]
        return carry

    lax.fori_loop(0, 4, turn, 0)
    nb_sib = peer(0, z, 1 - c)
    nb_z = peer(0, 1 - z, c)
    nb_diag = peer(0, 1 - z, 1 - c)
    send(nbt.at[nb_sib], nbq.at[quad], nb_ss.at[0], nb_rs.at[0], sib)
    nbq[quad] = nbt[quad]

    def ordering(route_ref):
        st = (route_ref[...] == lax.broadcasted_iota(jnp.int32, (PEERS, PEERS), 1)).astype(F32).astype(BF16)
        e = ((lax.broadcasted_iota(jnp.int32, (TOK, PEERS), 0) >> 4)
             == lax.broadcasted_iota(jnp.int32, (TOK, PEERS), 1)).astype(F32).astype(BF16)
        er = dot(e, st, ((1,), (1,))).astype(BF16)
        full = dot(er, e, ((1,), (1,)))
        same = (lax.broadcasted_iota(jnp.int32, (TOK, TOK), 0) & 15) == (
            lax.broadcasted_iota(jnp.int32, (TOK, TOK), 1) & 15)
        return jnp.where(same, full, 0.0).astype(BF16)

    def reorder(order, src, dst):
        def body(i, carry):
            cols = pl.ds(pl.multiple_of(i * TILE, TILE), TILE)
            dst[:, cols] = dot(order, src[:, cols], ((1,), (0,))).astype(BF16)
            return carry

        lax.fori_loop(0, C // TILE, body, 0)

    loads[1].wait()
    reorder(ordering(froute), af, aperm)

    def norm_a(i, carry):
        r = pl.ds(pl.multiple_of(i * 16, 16), 16)
        wide = aperm[r].astype(F32)
        rstd = lax.rsqrt(jnp.mean(wide * wide, axis=-1, keepdims=True) + EPS)
        na[r] = (wide * rstd * gain[...]).astype(BF16)
        return carry

    lax.fori_loop(0, TOK // 16, norm_a, 0)
    order_b = ordering(broute)
    reorder(order_b, ab, bperm)
    loads[2].wait()
    reorder(order_b, cotq.at[own_slot], cperm)
    loads[3].wait()

    ag_wait(rows(x, 1 - z), 0)
    ag_send(rows(x, 1 - z), rows(x, 1 - z), 3, 2, right)
    ag_send(rows(x, 1 - z), rows(x, 1 - z), 4, 6, left)
    sib_send(rows(x, 1 - z), rows(x, 1 - z), 1)
    send(cot, cotq.at[own_slot], ex_ss.at[1], ex_rs.at[1], zpart)
    send(nbt.at[nb_z], nbq.at[quad], nb_ss.at[1], nb_rs.at[1], zpart)
    send(nbt.at[nb_diag], nbq.at[quad], nb_ss.at[2], nb_rs.at[2], diag)

    ag_wait(rows(xl, z), 1)
    ag_send(rows(xl, z, 0, HALF), rows(xl, z, 0, HALF), 5, 3, right)
    sib_send(rows(xl, z), rows(xl, z), 2)
    ag_wait(rows(xr, z), 5)
    ag_send(rows(xr, z, HALF, HALF), rows(xr, z, HALF, HALF), 6, 7, left)
    sib_send(rows(xr, z), rows(xr, z), 3)

    def base_of(px):
        return pl.multiple_of(px * GRP, GRP)

    def hidden_group(px, first, last):
        base = base_of(px)

        def body(i, carry):
            cols = pl.ds(pl.multiple_of(i * TILE, TILE), TILE)
            part = dot(na[:, pl.ds(base, GRP)], wg[pl.ds(base, GRP), cols], ((1,), (0,)))
            if not first:
                part = part + hacc[:, cols]
            if last:
                ostage[:, cols] = (aperm[:, cols].astype(F32) + part).astype(BF16)
            else:
                hacc[:, cols] = part
            return carry

        lax.fori_loop(0, C // TILE, body, 0)

    def grad_group(px):
        base = base_of(px)

        def body(i, carry):
            at = pl.multiple_of(base + i * 128, 128)
            gn[:, pl.ds(at, 128)] = dot(cperm[...], wg[pl.ds(at, 128)], ((1,), (1,)))
            return carry

        lax.fori_loop(0, GRP // 128, body, 0)

    sib_wait(x, z, 0)
    sib_wait(x, 1 - z, 1)
    hidden_group(x, True, False)
    grad_group(x)

    ag_wait(rows(xl, 1 - z), 2)
    ag_send(rows(xl, 1 - z, 0, HALF), rows(xl, 1 - z, 0, HALF), 7, 4, right)
    sib_send(rows(xl, 1 - z), rows(xl, 1 - z), 4)
    ag_wait(rows(xr, 1 - z), 6)
    ag_send(rows(xr, 1 - z, HALF, HALF), rows(xr, 1 - z, HALF, HALF), 8, 8, left)
    sib_send(rows(xr, 1 - z), rows(xr, 1 - z), 5)

    sib_wait(xl, z, 2)
    sib_wait(xl, 1 - z, 4)
    hidden_group(xl, False, False)
    grad_group(xl)
    sib_wait(xr, z, 3)
    sib_wait(xr, 1 - z, 5)
    hidden_group(xr, False, False)
    grad_group(xr)

    ag_wait(rows(x2, z, 0, HALF), 3)
    sib_send(rows(x2, z, 0, HALF), rows(x2, z, 0, HALF), 6)
    ag_wait(rows(x2, z, HALF, HALF), 7)
    sib_send(rows(x2, z, HALF, HALF), rows(x2, z, HALF, HALF), 7)
    ag_wait(rows(x2, 1 - z, 0, HALF), 4)
    sib_send(rows(x2, 1 - z, 0, HALF), rows(x2, 1 - z, 0, HALF), 8)
    ag_wait(rows(x2, 1 - z, HALF, HALF), 8)
    sib_send(rows(x2, 1 - z, HALF, HALF), rows(x2, 1 - z, HALF, HALF), 9)
    sib_wait(x2, z, 6, 0, HALF)
    sib_wait(x2, z, 7, HALF, HALF)
    sib_wait(x2, 1 - z, 8, 0, HALF)
    sib_wait(x2, 1 - z, 9, HALF, HALF)

    hidden_group(x2, False, True)

    def deal(stage, out, k, section):
        def body(i, carry):
            p = lax.rem(q + i, PEERS)
            remote(
                stage.at[pl.ds(pl.multiple_of(p * BLK, BLK), BLK)],
                out.at[pl.ds(pl.multiple_of(q * BLK, BLK), BLK)],
                a2a_ss.at[k], a2a_rs.at[k], (section, p),
            ).start()
            return carry

        lax.fori_loop(0, PEERS, body, 0)

    @pl.when(s < SECTIONS - 1)
    def _():
        deal(ostage, next_o, 0, up)

    grad_group(x2)

    def grad_rows(i, carry):
        r = pl.ds(pl.multiple_of(i * 16, 16), 16)
        wide = bperm[r].astype(F32)
        rstd = lax.rsqrt(jnp.mean(wide * wide, axis=-1, keepdims=True) + EPS)
        scaled = gain[...] * gn[r]
        inner = jnp.mean(wide * scaled, axis=-1, keepdims=True)
        gstage[r] = (cperm[r].astype(F32) + rstd * scaled - wide * (rstd * rstd * rstd * inner)).astype(BF16)
        return carry

    lax.fori_loop(0, TOK // 16, grad_rows, 0)

    @pl.when(s > 0)
    def _():
        deal(gstage, back_o, 1, down)

    def slot(pz, pc):
        return cotq.at[pl.ds(pl.multiple_of(peer(0, pz, pc) * TOK, TOK), TOK)]

    def ex_wait(region, k):
        remote(region, region, ex_ss.at[0], ex_rs.at[k], sib).wait_recv()

    ex_wait(slot(1 - z, c), 1)
    send(slot(1 - z, c), slot(1 - z, c), ex_ss.at[2], ex_rs.at[2], sib)
    ex_wait(slot(z, 1 - c), 0)
    for k, src in enumerate((nb_sib, nb_z, nb_diag)):
        remote(nbq.at[src], nbq.at[src], nb_ss.at[0], nb_rs.at[k], sib).wait_recv()
    ex_wait(slot(1 - z, 1 - c), 2)

    def partial(px, cols):
        r = pl.ds(pl.multiple_of(px * SH, SH), SH)
        acc = dot(nbq[0, r], cotq[pl.ds(0, TOK), cols], ((1,), (0,)))
        for k in range(1, 4):
            acc = acc + dot(nbq[k, r], cotq[pl.ds(k * TOK, TOK), cols], ((1,), (0,)))
        return acc

    def partial_to(px, k):
        def body(i, carry):
            cols = pl.ds(pl.multiple_of(i * TILE, TILE), TILE)
            psend[k, :, cols] = partial(px, cols).astype(BF16)
            return carry

        lax.fori_loop(0, C // TILE, body, 0)

    first = pl.ds(0, HALF)
    second = pl.ds(HALF, HALF)
    partial_to(x2, 0)
    send(psend.at[0, first], rs_half.at[0], red_ss.at[0], red_rs.at[0], right)
    send(psend.at[0, second], rs_half.at[1], red_ss.at[1], red_rs.at[1], left)
    partial_to(xr, 1)
    send(psend.at[1, second], rs_full.at[0, second], red_ss.at[2], red_rs.at[3], right)
    partial_to(xl, 2)
    send(psend.at[2, first], rs_full.at[1, first], red_ss.at[3], red_rs.at[4], left)

    def own(i, carry):
        cols = pl.ds(pl.multiple_of(i * TILE, TILE), TILE)
        dw_o[:, cols] = partial(x, cols)
        return carry

    lax.fori_loop(0, C // TILE, own, 0)

    def add_half(k, half, region):
        def body(i, carry):
            r = pl.ds(pl.multiple_of(i * 16, 16), 16)
            at = pl.ds(pl.multiple_of(half * HALF + i * 16, 16), 16)
            psend[k, at] = (psend[k, at].astype(F32) + rs_half[half, r].astype(F32)).astype(BF16)
            return carry

        lax.fori_loop(0, HALF // 16, body, 0)

    remote(rs_half.at[0], rs_half.at[0], red_ss.at[0], red_rs.at[0], left).wait_recv()
    add_half(1, 0, first)
    send(psend.at[1, first], rs_full.at[0, first], red_ss.at[4], red_rs.at[2], right)
    remote(rs_half.at[1], rs_half.at[1], red_ss.at[0], red_rs.at[1], right).wait_recv()
    add_half(2, 1, second)
    send(psend.at[2, second], rs_full.at[1, second], red_ss.at[5], red_rs.at[5], left)

    for side in range(2):
        for h, part in enumerate((first, second)):
            region = rs_full.at[side, part]
            remote(region, region, red_ss.at[0], red_rs.at[2 + 2 * side + h], left).wait_recv()

    def finish(i, carry):
        r = pl.ds(pl.multiple_of(i * 16, 16), 16)
        dw_o[r] = (dw_o[r] + rs_full[0, r].astype(F32) + rs_full[1, r].astype(F32)) / count
        return carry

    lax.fori_loop(0, SH // 16, finish, 0)

    for cp in sent:
        cp.wait_send()

    @pl.when(s < SECTIONS - 1)
    def _():
        remote(ostage, next_o, a2a_ss.at[0], a2a_rs.at[0], sib).wait_send()

    @pl.when(s > 0)
    def _():
        remote(gstage, back_o, a2a_ss.at[1], a2a_rs.at[1], sib).wait_send()

    @pl.when(s > 0)
    def _():
        remote(ostage, next_o, a2a_ss.at[0], a2a_rs.at[0], sib).wait_recv()

    @pl.when(s < SECTIONS - 1)
    def _():
        remote(gstage, back_o, a2a_ss.at[1], a2a_rs.at[1], sib).wait_recv()

    @pl.when(s == 0)
    def _():
        nb[...] = jnp.zeros_like(nb)
        cp = pltpu.make_async_copy(nb, next_o, loc_sem.at[0])
        cp.start()
        cp.wait()

    @pl.when(s == SECTIONS - 1)
    def _():
        nb[...] = jnp.zeros_like(nb)
        cp = pltpu.make_async_copy(nb, back_o, loc_sem.at[0])
        cp.start()
        cp.wait()


def local(acts_fwd, acts_bwd, cot_bwd, gain, proj, fwd_route, bwd_route, straggler):
    hbm = pl.BlockSpec(memory_space=pl.ANY)
    vmem = pl.BlockSpec(memory_space=pltpu.VMEM)
    smem = pl.BlockSpec(memory_space=pltpu.SMEM)
    dma = pltpu.SemaphoreType.DMA
    out = pl.pallas_call(
        kernel,
        name="swarm_tick",
        out_shape=(
            jax.ShapeDtypeStruct((TOK, C), BF16),
            jax.ShapeDtypeStruct((TOK, C), BF16),
            jax.ShapeDtypeStruct((SH, C), F32),
        ),
        in_specs=[hbm, hbm, hbm, vmem, hbm, vmem, vmem, smem],
        out_specs=(hbm, hbm, vmem),
        scratch_shapes=[
            pltpu.VMEM((C, C), BF16),
            pltpu.VMEM((TOK, C), BF16),
            pltpu.VMEM((TOK, C), BF16),
            pltpu.VMEM((TOK, C), BF16),
            pltpu.VMEM((TOK, C), BF16),
            pltpu.VMEM((TOK, C), BF16),
            pltpu.VMEM((TOK, C), BF16),
            pltpu.VMEM((TOK, C), BF16),
            pltpu.VMEM((4, GRP, TOK), BF16),
            pltpu.VMEM((4, GRP, TOK), BF16),
            pltpu.VMEM((4 * TOK, C), BF16),
            pltpu.VMEM((TOK, C), F32),
            pltpu.VMEM((TOK, C), F32),
            pltpu.VMEM((TOK, C), BF16),
            pltpu.VMEM((TOK, C), BF16),
            pltpu.VMEM((3, SH, C), BF16),
            pltpu.VMEM((2, HALF, C), BF16),
            pltpu.VMEM((2, SH, C), BF16),
            dma((4,)),
            dma((9,)), dma((9,)),
            dma((10,)), dma((10,)),
            dma((3,)), dma((3,)),
            dma((3,)), dma((3,)),
            dma((6,)), dma((6,)),
            dma((2,)), dma((2,)),
        ],
        compiler_params=pltpu.CompilerParams(
            collective_id=0, has_side_effects=True, vmem_limit_bytes=56 * 2**20
        ),
        cost_estimate=pl.CostEstimate(
            flops=6 * TOK * C * C, bytes_accessed=20 * 2**20, transcendentals=0
        ),
    )(
        acts_fwd[0], acts_bwd[0], cot_bwd[0], gain, proj[0], fwd_route[0], bwd_route[0], straggler
    )
    return tuple(o[None] for o in out)


def solution(mesh):
    split = P("section", "peer", None)
    whole = P("section", None)
    return jax.shard_map(
        local,
        mesh=mesh,
        in_specs=(split, split, split, whole, split, split, split, whole),
        out_specs=(split, split, split),
        check_vma=False,
    )
```

```python
import jax
import jax.numpy as jnp
from jax import lax
from jax.experimental import pallas as pl
from jax.experimental.pallas import tpu as pltpu
from jax.sharding import PartitionSpec as P

MESH = pl.DeviceIdType.MESH
F32 = jnp.float32
BF16 = jnp.bfloat16
EPS = 1e-05
START = 7
STRIDE = 1

SECTIONS = 16
PEERS = 16
C = 2560
TOK = 256
BLK = 16
SH = C // PEERS
HALF = SH // 2
GRP = 4 * SH
TILE = 512


def dot(a, b, dims):
    return lax.dot_general(a, b, (dims, ((), ())), preferred_element_type=F32)


def kernel(
    acts_f, acts_b, cot, gain, proj, froute, broute, strag,
    next_o, back_o, dw_o,
    wg, af, ab, aperm, bperm, cperm, na, nb, nbt, nbq, cotq, hacc, gn, ostage, gstage,
    psend, rs_half, rs_full,
    loc_sem, ag_ss, ag_rs, sib_ss, sib_rs, ex_ss, ex_rs, nb_ss, nb_rs, red_ss, red_rs, a2a_ss, a2a_rs, ready,
):
    s = lax.axis_index("section")
    q = lax.axis_index("peer")
    x = lax.div(q, 4)
    quad = lax.rem(q, 4)
    z = lax.div(quad, 2)
    c = lax.rem(q, 2)
    xr = lax.rem(x + 1, 4)
    xl = lax.rem(x + 3, 4)
    x2 = lax.rem(x + 2, 4)
    up = lax.rem(s + 1, SECTIONS)
    down = lax.rem(s + SECTIONS - 1, SECTIONS)

    def peer(px, pz, pc):
        return px * 4 + pz * 2 + pc

    right = (s, peer(xr, z, c))
    left = (s, peer(xl, z, c))
    zpart = (s, peer(x, 1 - z, c))
    sib = (s, peer(x, z, 1 - c))
    diag = (s, peer(x, 1 - z, 1 - c))

    bar = pltpu.get_barrier_semaphore()
    for dev in (right, left, zpart, sib, diag, (up, q), (down, q)):
        pl.semaphore_signal(bar, inc=1, device_id=dev, device_id_type=MESH)
    pl.semaphore_wait(bar, 7)

    def remote(src, dst, ss, rs, dev):
        return pltpu.make_async_remote_copy(
            src_ref=src, dst_ref=dst, send_sem=ss, recv_sem=rs, device_id=dev, device_id_type=MESH
        )

    def rows(px, pz, lo=0, n=SH, pc=c):
        return wg.at[pl.ds(pl.multiple_of(peer(px, pz, pc) * SH + lo, 16), n)]

    sent = []

    def send(src, dst, ss, rs, dev):
        cp = remote(src, dst, ss, rs, dev)
        cp.start()
        sent.append(cp)

    def ag_send(src, region, k_send, k_recv, dev):
        send(src, region, ag_ss.at[k_send], ag_rs.at[k_recv], dev)

    def ag_wait(region, k_recv):
        remote(region, region, ag_ss.at[0], ag_rs.at[k_recv], zpart).wait_recv()

    def sib_send(src, region, k):
        send(src, region, sib_ss.at[k], sib_rs.at[k], sib)

    def sib_wait(px, pz, k, lo=0, n=SH):
        region = rows(px, pz, lo, n, 1 - c)
        remote(region, region, sib_ss.at[k], sib_rs.at[k], sib).wait_recv()

    ag_send(proj, rows(x, z), 0, 0, zpart)
    ag_send(proj, rows(x, z), 1, 1, right)
    ag_send(proj, rows(x, z), 2, 5, left)
    sib_send(proj, rows(x, z), 0)
    own_slot = pl.ds(pl.multiple_of(quad * TOK, TOK), TOK)
    loads = [
        pltpu.make_async_copy(acts_b, ab, loc_sem.at[0]),
        pltpu.make_async_copy(acts_f, af, loc_sem.at[1]),
        pltpu.make_async_copy(cot, cotq.at[own_slot], loc_sem.at[2]),
        pltpu.make_async_copy(proj, rows(x, z), loc_sem.at[3]),
    ]
    for cp in loads:
        cp.start()
    send(cot, cotq.at[own_slot], ex_ss.at[0], ex_rs.at[0], sib)

    count = jnp.float32(0)
    for i in range(PEERS):
        count = count + (1 - strag[0, i]).astype(F32)
    keep = (1 - strag[0, q]).astype(F32)

    loads[0].wait()

    def norm_b(i, carry):
        r = pl.ds(pl.multiple_of(i * 16, 16), 16)
        wide = ab[r].astype(F32)
        rstd = lax.rsqrt(jnp.mean(wide * wide, axis=-1, keepdims=True) + EPS)
        nb[r] = (wide * rstd * gain[...] * keep).astype(BF16)
        return carry

    lax.fori_loop(0, TOK // 16, norm_b, 0)

    def turn(i, carry):
        cols = pl.ds(pl.multiple_of(i * GRP, GRP), GRP)
        t = nb[:, cols].T
        for k in range(4):
            nbt[k, pl.ds(pl.multiple_of(i * SH, SH), SH)] = t[k * SH:(k + 1) * SH]
        return carry

    lax.fori_loop(0, 4, turn, 0)
    nb_sib = peer(0, z, 1 - c)
    nb_z = peer(0, 1 - z, c)
    nb_diag = peer(0, 1 - z, 1 - c)
    send(nbt.at[nb_sib], nbq.at[quad], nb_ss.at[0], nb_rs.at[0], sib)
    nbq[quad] = nbt[quad]

    def ordering(route_ref):
        st = (route_ref[...] == lax.broadcasted_iota(jnp.int32, (PEERS, PEERS), 0)).astype(F32).astype(BF16)
        e = ((lax.broadcasted_iota(jnp.int32, (TOK, PEERS), 0) >> 4)
             == lax.broadcasted_iota(jnp.int32, (TOK, PEERS), 1)).astype(F32).astype(BF16)
        er = dot(e, st, ((1,), (0,))).astype(BF16)
        full = dot(er, e, ((1,), (1,)))
        same = (lax.broadcasted_iota(jnp.int32, (TOK, TOK), 0) & 15) == (
            lax.broadcasted_iota(jnp.int32, (TOK, TOK), 1) & 15)
        return jnp.where(same, full, 0.0).astype(BF16)

    def reorder(order, src, dst):
        def body(i, carry):
            cols = pl.ds(pl.multiple_of(i * TILE, TILE), TILE)
            dst[:, cols] = dot(order, src[:, cols], ((1,), (0,))).astype(BF16)
            return carry

        lax.fori_loop(0, C // TILE, body, 0)

    loads[1].wait()
    reorder(ordering(froute), af, aperm)

    def norm_a(i, carry):
        r = pl.ds(pl.multiple_of(i * 16, 16), 16)
        wide = aperm[r].astype(F32)
        rstd = lax.rsqrt(jnp.mean(wide * wide, axis=-1, keepdims=True) + EPS)
        na[r] = (wide * rstd * gain[...]).astype(BF16)
        return carry

    lax.fori_loop(0, TOK // 16, norm_a, 0)
    order_b = ordering(broute)
    reorder(order_b, ab, bperm)
    loads[2].wait()
    reorder(order_b, cotq.at[own_slot], cperm)
    loads[3].wait()

    @pl.when(s == 0)
    def _():
        ostage[...] = jnp.zeros_like(ostage)
        zeros = pltpu.make_async_copy(ostage, next_o, loc_sem.at[0])
        zeros.start()
        zeros.wait()

    @pl.when(s == SECTIONS - 1)
    def _():
        gstage[...] = jnp.zeros_like(gstage)
        zeros = pltpu.make_async_copy(gstage, back_o, loc_sem.at[0])
        zeros.start()
        zeros.wait()

    ag_wait(rows(x, 1 - z), 0)
    ag_send(rows(x, 1 - z), rows(x, 1 - z), 3, 2, right)
    ag_send(rows(x, 1 - z), rows(x, 1 - z), 4, 6, left)
    sib_send(rows(x, 1 - z), rows(x, 1 - z), 1)
    send(cot, cotq.at[own_slot], ex_ss.at[1], ex_rs.at[1], zpart)
    send(nbt.at[nb_z], nbq.at[quad], nb_ss.at[1], nb_rs.at[1], zpart)
    send(nbt.at[nb_diag], nbq.at[quad], nb_ss.at[2], nb_rs.at[2], diag)

    ag_wait(rows(xl, z), 1)
    ag_send(rows(xl, z, 0, HALF), rows(xl, z, 0, HALF), 5, 3, right)
    sib_send(rows(xl, z), rows(xl, z), 2)
    ag_wait(rows(xr, z), 5)
    ag_send(rows(xr, z, HALF, HALF), rows(xr, z, HALF, HALF), 6, 7, left)
    sib_send(rows(xr, z), rows(xr, z), 3)

    def base_of(px):
        return pl.multiple_of(px * GRP, GRP)

    def hidden_group(px, first, last):
        base = base_of(px)

        def body(i, carry):
            cols = pl.ds(pl.multiple_of(i * TILE, TILE), TILE)
            part = dot(na[:, pl.ds(base, GRP)], wg[pl.ds(base, GRP), cols], ((1,), (0,)))
            if not first:
                part = part + hacc[:, cols]
            if last:
                ostage[:, cols] = (aperm[:, cols].astype(F32) + part).astype(BF16)
            else:
                hacc[:, cols] = part
            return carry

        lax.fori_loop(0, C // TILE, body, 0)

    def grad_group(px):
        base = base_of(px)

        def body(i, carry):
            at = pl.multiple_of(base + i * 128, 128)
            gn[:, pl.ds(at, 128)] = dot(cperm[...], wg[pl.ds(at, 128)], ((1,), (1,)))
            return carry

        lax.fori_loop(0, GRP // 128, body, 0)

    sib_wait(x, z, 0)
    sib_wait(x, 1 - z, 1)
    hidden_group(x, True, False)
    grad_group(x)

    ag_wait(rows(xl, 1 - z), 2)
    ag_send(rows(xl, 1 - z, 0, HALF), rows(xl, 1 - z, 0, HALF), 7, 4, right)
    sib_send(rows(xl, 1 - z), rows(xl, 1 - z), 4)
    ag_wait(rows(xr, 1 - z), 6)
    ag_send(rows(xr, 1 - z, HALF, HALF), rows(xr, 1 - z, HALF, HALF), 8, 8, left)
    sib_send(rows(xr, 1 - z), rows(xr, 1 - z), 5)

    sib_wait(xl, z, 2)
    sib_wait(xl, 1 - z, 4)
    hidden_group(xl, False, False)
    grad_group(xl)
    sib_wait(xr, z, 3)
    sib_wait(xr, 1 - z, 5)
    hidden_group(xr, False, False)
    grad_group(xr)

    ag_wait(rows(x2, z, 0, HALF), 3)
    sib_send(rows(x2, z, 0, HALF), rows(x2, z, 0, HALF), 6)
    ag_wait(rows(x2, z, HALF, HALF), 7)
    sib_send(rows(x2, z, HALF, HALF), rows(x2, z, HALF, HALF), 7)
    ag_wait(rows(x2, 1 - z, 0, HALF), 4)
    sib_send(rows(x2, 1 - z, 0, HALF), rows(x2, 1 - z, 0, HALF), 8)
    ag_wait(rows(x2, 1 - z, HALF, HALF), 8)
    sib_send(rows(x2, 1 - z, HALF, HALF), rows(x2, 1 - z, HALF, HALF), 9)
    sib_wait(x2, z, 6, 0, HALF)
    sib_wait(x2, z, 7, HALF, HALF)
    sib_wait(x2, 1 - z, 8, 0, HALF)
    sib_wait(x2, 1 - z, 9, HALF, HALF)

    pl.semaphore_signal(ready.at[0], inc=1, device_id=(down, q), device_id_type=MESH)
    pl.semaphore_signal(ready.at[1], inc=1, device_id=(up, q), device_id_type=MESH)

    hidden_group(x2, False, True)
    pl.semaphore_wait(ready.at[0], 1)

    def send_block(stage, out, k, section, p):
        remote(
            stage.at[pl.ds(pl.multiple_of(p * BLK, BLK), BLK)],
            out.at[pl.ds(pl.multiple_of(q * BLK, BLK), BLK)],
            a2a_ss.at[k], a2a_rs.at[k], (section, p),
        ).start()

    @pl.when(s < SECTIONS - 1)
    def _():
        def deal(i, carry):
            send_block(ostage, next_o, 0, up, lax.rem(q + START + STRIDE * i, PEERS))
            return carry

        lax.fori_loop(0, PEERS, deal, 0)

    grad_group(x2)
    pl.semaphore_wait(ready.at[1], 1)

    def grad_rows(i, carry):
        p = lax.rem(q + START + STRIDE * i, PEERS)
        r = pl.ds(pl.multiple_of(p * BLK, BLK), BLK)
        wide = bperm[r].astype(F32)
        rstd = lax.rsqrt(jnp.mean(wide * wide, axis=-1, keepdims=True) + EPS)
        scaled = gain[...] * gn[r]
        inner = jnp.mean(wide * scaled, axis=-1, keepdims=True)
        gstage[r] = (cperm[r].astype(F32) + rstd * scaled - wide * (rstd * rstd * rstd * inner)).astype(BF16)

        @pl.when(s > 0)
        def _():
            send_block(gstage, back_o, 1, down, p)

        return carry

    lax.fori_loop(0, PEERS, grad_rows, 0)

    def slot(pz, pc):
        return cotq.at[pl.ds(pl.multiple_of(peer(0, pz, pc) * TOK, TOK), TOK)]

    def ex_wait(region, k):
        remote(region, region, ex_ss.at[0], ex_rs.at[k], sib).wait_recv()

    ex_wait(slot(1 - z, c), 1)
    send(slot(1 - z, c), slot(1 - z, c), ex_ss.at[2], ex_rs.at[2], sib)
    ex_wait(slot(z, 1 - c), 0)
    for k, src in enumerate((nb_sib, nb_z, nb_diag)):
        remote(nbq.at[src], nbq.at[src], nb_ss.at[0], nb_rs.at[k], sib).wait_recv()
    ex_wait(slot(1 - z, 1 - c), 2)

    def partial(px, cols):
        r = pl.ds(pl.multiple_of(px * SH, SH), SH)
        acc = dot(nbq[0, r], cotq[pl.ds(0, TOK), cols], ((1,), (0,)))
        for k in range(1, 4):
            acc = acc + dot(nbq[k, r], cotq[pl.ds(k * TOK, TOK), cols], ((1,), (0,)))
        return acc

    def partial_to(px, k):
        def body(i, carry):
            cols = pl.ds(pl.multiple_of(i * TILE, TILE), TILE)
            psend[k, :, cols] = partial(px, cols).astype(BF16)
            return carry

        lax.fori_loop(0, C // TILE, body, 0)

    first = pl.ds(0, HALF)
    second = pl.ds(HALF, HALF)
    partial_to(x2, 0)
    send(psend.at[0, first], rs_half.at[0], red_ss.at[0], red_rs.at[0], right)
    send(psend.at[0, second], rs_half.at[1], red_ss.at[1], red_rs.at[1], left)
    partial_to(xr, 1)
    send(psend.at[1, second], rs_full.at[0, second], red_ss.at[2], red_rs.at[3], right)
    partial_to(xl, 2)
    send(psend.at[2, first], rs_full.at[1, first], red_ss.at[3], red_rs.at[4], left)

    def own(i, carry):
        cols = pl.ds(pl.multiple_of(i * TILE, TILE), TILE)
        dw_o[:, cols] = partial(x, cols)
        return carry

    lax.fori_loop(0, C // TILE, own, 0)

    def add_half(k, half, region):
        def body(i, carry):
            r = pl.ds(pl.multiple_of(i * 16, 16), 16)
            at = pl.ds(pl.multiple_of(half * HALF + i * 16, 16), 16)
            psend[k, at] = (psend[k, at].astype(F32) + rs_half[half, r].astype(F32)).astype(BF16)
            return carry

        lax.fori_loop(0, HALF // 16, body, 0)

    remote(rs_half.at[0], rs_half.at[0], red_ss.at[0], red_rs.at[0], left).wait_recv()
    add_half(1, 0, first)
    send(psend.at[1, first], rs_full.at[0, first], red_ss.at[4], red_rs.at[2], right)
    remote(rs_half.at[1], rs_half.at[1], red_ss.at[0], red_rs.at[1], right).wait_recv()
    add_half(2, 1, second)
    send(psend.at[2, second], rs_full.at[1, second], red_ss.at[5], red_rs.at[5], left)

    for side in range(2):
        for h, part in enumerate((first, second)):
            region = rs_full.at[side, part]
            remote(region, region, red_ss.at[0], red_rs.at[2 + 2 * side + h], left).wait_recv()

    def finish(i, carry):
        r = pl.ds(pl.multiple_of(i * 16, 16), 16)
        dw_o[r] = (dw_o[r] + rs_full[0, r].astype(F32) + rs_full[1, r].astype(F32)) / count
        return carry

    lax.fori_loop(0, SH // 16, finish, 0)

    for cp in sent:
        cp.wait_send()

    @pl.when(s < SECTIONS - 1)
    def _():
        remote(ostage, next_o, a2a_ss.at[0], a2a_rs.at[0], sib).wait_send()

    @pl.when(s > 0)
    def _():
        remote(gstage, back_o, a2a_ss.at[1], a2a_rs.at[1], sib).wait_send()

    @pl.when(s > 0)
    def _():
        remote(ostage, next_o, a2a_ss.at[0], a2a_rs.at[0], sib).wait_recv()

    @pl.when(s < SECTIONS - 1)
    def _():
        remote(gstage, back_o, a2a_ss.at[1], a2a_rs.at[1], sib).wait_recv()


def local(acts_fwd, acts_bwd, cot_bwd, gain, proj, fwd_route, bwd_route, straggler):
    hbm = pl.BlockSpec(memory_space=pl.ANY)
    vmem = pl.BlockSpec(memory_space=pltpu.VMEM)
    smem = pl.BlockSpec(memory_space=pltpu.SMEM)
    dma = pltpu.SemaphoreType.DMA
    out = pl.pallas_call(
        kernel,
        name="swarm_tick",
        out_shape=(
            jax.ShapeDtypeStruct((TOK, C), BF16),
            jax.ShapeDtypeStruct((TOK, C), BF16),
            jax.ShapeDtypeStruct((SH, C), F32),
        ),
        in_specs=[hbm, hbm, hbm, vmem, hbm, vmem, vmem, smem],
        out_specs=(hbm, hbm, vmem),
        scratch_shapes=[
            pltpu.VMEM((C, C), BF16),
            pltpu.VMEM((TOK, C), BF16),
            pltpu.VMEM((TOK, C), BF16),
            pltpu.VMEM((TOK, C), BF16),
            pltpu.VMEM((TOK, C), BF16),
            pltpu.VMEM((TOK, C), BF16),
            pltpu.VMEM((TOK, C), BF16),
            pltpu.VMEM((TOK, C), BF16),
            pltpu.VMEM((4, GRP, TOK), BF16),
            pltpu.VMEM((4, GRP, TOK), BF16),
            pltpu.VMEM((4 * TOK, C), BF16),
            pltpu.VMEM((TOK, C), F32),
            pltpu.VMEM((TOK, C), F32),
            pltpu.VMEM((TOK, C), BF16),
            pltpu.VMEM((TOK, C), BF16),
            pltpu.VMEM((3, SH, C), BF16),
            pltpu.VMEM((2, HALF, C), BF16),
            pltpu.VMEM((2, SH, C), BF16),
            dma((4,)),
            dma((9,)), dma((9,)),
            dma((10,)), dma((10,)),
            dma((3,)), dma((3,)),
            dma((3,)), dma((3,)),
            dma((6,)), dma((6,)),
            dma((2,)), dma((2,)),
            pltpu.SemaphoreType.REGULAR((2,)),
        ],
        compiler_params=pltpu.CompilerParams(
            collective_id=0, has_side_effects=True, vmem_limit_bytes=56 * 2**20
        ),
        cost_estimate=pl.CostEstimate(
            flops=6 * TOK * C * C, bytes_accessed=20 * 2**20, transcendentals=0
        ),
    )(
        acts_fwd[0], acts_bwd[0], cot_bwd[0], gain, proj[0],
        fwd_route.reshape(1, PEERS), bwd_route.reshape(1, PEERS), straggler,
    )
    return write_out(*out)


PARTS = 4


def write_kernel(a, b, w, ao, bo, wo, av, bv, wv, in_sem, out_sem):
    moves = []
    for k in range(PARTS):
        for i, (src, buf, dst) in enumerate(((a, av, ao.at[0]), (b, bv, bo.at[0]), (w, wv, wo.at[0]))):
            n = src.shape[0] // PARTS
            at = pl.ds(k * n, n)
            moves.append((
                pltpu.make_async_copy(src.at[at], buf.at[at], in_sem.at[k, i]),
                pltpu.make_async_copy(buf.at[at], dst.at[at], out_sem.at[k, i]),
            ))
    for read, _ in moves:
        read.start()
    for read, write in moves:
        read.wait()
        write.start()
    for _, write in moves:
        write.wait()


def write_out(*results):
    any_spec = pl.BlockSpec(memory_space=pl.ANY)
    dma = pltpu.SemaphoreType.DMA
    return pl.pallas_call(
        write_kernel,
        name="write_out",
        out_shape=tuple(jax.ShapeDtypeStruct((1, *v.shape), v.dtype) for v in results),
        in_specs=[any_spec] * 3,
        out_specs=(any_spec,) * 3,
        scratch_shapes=[pltpu.VMEM(v.shape, v.dtype) for v in results] + [dma((PARTS, 3)), dma((PARTS, 3))],
        compiler_params=pltpu.CompilerParams(vmem_limit_bytes=56 * 2**20),
    )(*results)


def solution(mesh):
    split = P("section", "peer", None)
    whole = P("section", None)
    return jax.shard_map(
        local,
        mesh=mesh,
        in_specs=(split, split, split, whole, split, split, split, whole),
        out_specs=(split, split, split),
        check_vma=False,
    )
```

```python
import jax
import jax.numpy as jnp
from jax import lax
from jax.experimental import pallas as pl
from jax.experimental.pallas import tpu as pltpu
from jax.sharding import PartitionSpec as P

MESH = pl.DeviceIdType.MESH
F32 = jnp.float32
BF16 = jnp.bfloat16
EPS = 1e-05
START = 7
STRIDE = 1

SECTIONS = 16
PEERS = 16
C = 2560
TOK = 256
BLK = 16
SH = C // PEERS
HALF = SH // 2
GRP = 4 * SH
TILE = 512


def dot(a, b, dims):
    return lax.dot_general(a, b, (dims, ((), ())), preferred_element_type=F32)


def kernel(
    acts_f, acts_b, cot, gain, proj, froute, broute, strag,
    next_o, back_o, dw_o,
    wg, af, ab, aperm, bperm, cperm, na, nb, nbt, nbq, cotq, hacc, gn, ostage, gstage,
    psend, rs_half, rs_full,
    loc_sem, ag_ss, ag_rs, sib_ss, sib_rs, ex_ss, ex_rs, nb_ss, nb_rs, red_ss, red_rs, a2a_ss, a2a_rs, ready,
):
    s = lax.axis_index("section")
    q = lax.axis_index("peer")
    x = lax.div(q, 4)
    quad = lax.rem(q, 4)
    z = lax.div(quad, 2)
    c = lax.rem(q, 2)
    xr = lax.rem(x + 1, 4)
    xl = lax.rem(x + 3, 4)
    x2 = lax.rem(x + 2, 4)
    up = lax.rem(s + 1, SECTIONS)
    down = lax.rem(s + SECTIONS - 1, SECTIONS)

    def peer(px, pz, pc):
        return px * 4 + pz * 2 + pc

    right = (s, peer(xr, z, c))
    left = (s, peer(xl, z, c))
    zpart = (s, peer(x, 1 - z, c))
    sib = (s, peer(x, z, 1 - c))
    diag = (s, peer(x, 1 - z, 1 - c))

    bar = pltpu.get_barrier_semaphore()
    has_up = s < SECTIONS - 1
    has_down = s > 0
    for dev in (right, left, zpart, sib, diag):
        pl.semaphore_signal(bar, inc=1, device_id=dev, device_id_type=MESH)

    @pl.when(has_up)
    def _():
        pl.semaphore_signal(bar, inc=1, device_id=(up, q), device_id_type=MESH)

    @pl.when(has_down)
    def _():
        pl.semaphore_signal(bar, inc=1, device_id=(down, q), device_id_type=MESH)

    pl.semaphore_wait(bar, 5 + has_up.astype(jnp.int32) + has_down.astype(jnp.int32))

    def remote(src, dst, ss, rs, dev):
        return pltpu.make_async_remote_copy(
            src_ref=src, dst_ref=dst, send_sem=ss, recv_sem=rs, device_id=dev, device_id_type=MESH
        )

    def rows(px, pz, lo=0, n=SH, pc=c):
        return wg.at[pl.ds(pl.multiple_of(peer(px, pz, pc) * SH + lo, 16), n)]

    sent = []

    def send(src, dst, ss, rs, dev):
        cp = remote(src, dst, ss, rs, dev)
        cp.start()
        sent.append(cp)

    def ag_send(src, region, k_send, k_recv, dev):
        send(src, region, ag_ss.at[k_send], ag_rs.at[k_recv], dev)

    def ag_wait(region, k_recv):
        remote(region, region, ag_ss.at[0], ag_rs.at[k_recv], zpart).wait_recv()

    def sib_send(src, region, k):
        send(src, region, sib_ss.at[k], sib_rs.at[k], sib)

    def sib_wait(px, pz, k, lo=0, n=SH):
        region = rows(px, pz, lo, n, 1 - c)
        remote(region, region, sib_ss.at[k], sib_rs.at[k], sib).wait_recv()

    ag_send(proj, rows(x, z), 0, 0, zpart)
    ag_send(proj, rows(x, z), 1, 1, right)
    ag_send(proj, rows(x, z), 2, 5, left)
    sib_send(proj, rows(x, z), 0)
    own_slot = pl.ds(pl.multiple_of(quad * TOK, TOK), TOK)
    loads = [
        pltpu.make_async_copy(acts_b, ab, loc_sem.at[0]),
        pltpu.make_async_copy(acts_f, af, loc_sem.at[1]),
        pltpu.make_async_copy(cot, cotq.at[own_slot], loc_sem.at[2]),
        pltpu.make_async_copy(proj, rows(x, z), loc_sem.at[3]),
    ]
    for cp in loads:
        cp.start()
    send(cot, cotq.at[own_slot], ex_ss.at[0], ex_rs.at[0], sib)

    count = jnp.float32(0)
    for i in range(PEERS):
        count = count + (1 - strag[0, i]).astype(F32)
    keep = (1 - strag[0, q]).astype(F32)

    loads[0].wait()

    def norm_b(i, carry):
        r = pl.ds(pl.multiple_of(i * 16, 16), 16)
        wide = ab[r].astype(F32)
        rstd = lax.rsqrt(jnp.mean(wide * wide, axis=-1, keepdims=True) + EPS)
        nb[r] = (wide * rstd * gain[...] * keep).astype(BF16)
        return carry

    lax.fori_loop(0, TOK // 16, norm_b, 0)

    def turn(i, carry):
        cols = pl.ds(pl.multiple_of(i * GRP, GRP), GRP)
        t = nb[:, cols].T
        for k in range(4):
            nbt[k, pl.ds(pl.multiple_of(i * SH, SH), SH)] = t[k * SH:(k + 1) * SH]
        return carry

    lax.fori_loop(0, 4, turn, 0)
    nb_sib = peer(0, z, 1 - c)
    nb_z = peer(0, 1 - z, c)
    nb_diag = peer(0, 1 - z, 1 - c)
    send(nbt.at[nb_sib], nbq.at[quad], nb_ss.at[0], nb_rs.at[0], sib)
    nbq[quad] = nbt[quad]

    def ordering(route_ref):
        st = (route_ref[...] == lax.broadcasted_iota(jnp.int32, (PEERS, PEERS), 0)).astype(F32).astype(BF16)
        e = ((lax.broadcasted_iota(jnp.int32, (TOK, PEERS), 0) >> 4)
             == lax.broadcasted_iota(jnp.int32, (TOK, PEERS), 1)).astype(F32).astype(BF16)
        er = dot(e, st, ((1,), (0,))).astype(BF16)
        full = dot(er, e, ((1,), (1,)))
        same = (lax.broadcasted_iota(jnp.int32, (TOK, TOK), 0) & 15) == (
            lax.broadcasted_iota(jnp.int32, (TOK, TOK), 1) & 15)
        return jnp.where(same, full, 0.0).astype(BF16)

    def reorder(order, src, dst):
        def body(i, carry):
            cols = pl.ds(pl.multiple_of(i * TILE, TILE), TILE)
            dst[:, cols] = dot(order, src[:, cols], ((1,), (0,))).astype(BF16)
            return carry

        lax.fori_loop(0, C // TILE, body, 0)

    loads[1].wait()
    reorder(ordering(froute), af, aperm)

    def norm_a(i, carry):
        r = pl.ds(pl.multiple_of(i * 16, 16), 16)
        wide = aperm[r].astype(F32)
        rstd = lax.rsqrt(jnp.mean(wide * wide, axis=-1, keepdims=True) + EPS)
        na[r] = (wide * rstd * gain[...]).astype(BF16)
        return carry

    lax.fori_loop(0, TOK // 16, norm_a, 0)
    order_b = ordering(broute)
    reorder(order_b, ab, bperm)
    loads[2].wait()
    reorder(order_b, cotq.at[own_slot], cperm)
    loads[3].wait()

    @pl.when(s == 0)
    def _():
        ostage[...] = jnp.zeros_like(ostage)
        zeros = pltpu.make_async_copy(ostage, next_o, loc_sem.at[0])
        zeros.start()
        zeros.wait()

    @pl.when(s == SECTIONS - 1)
    def _():
        gstage[...] = jnp.zeros_like(gstage)
        zeros = pltpu.make_async_copy(gstage, back_o, loc_sem.at[0])
        zeros.start()
        zeros.wait()

    ag_wait(rows(x, 1 - z), 0)
    ag_send(rows(x, 1 - z), rows(x, 1 - z), 3, 2, right)
    ag_send(rows(x, 1 - z), rows(x, 1 - z), 4, 6, left)
    sib_send(rows(x, 1 - z), rows(x, 1 - z), 1)
    send(cot, cotq.at[own_slot], ex_ss.at[1], ex_rs.at[1], zpart)
    send(nbt.at[nb_z], nbq.at[quad], nb_ss.at[1], nb_rs.at[1], zpart)
    send(nbt.at[nb_diag], nbq.at[quad], nb_ss.at[2], nb_rs.at[2], diag)

    ag_wait(rows(xl, z), 1)
    ag_send(rows(xl, z, 0, HALF), rows(xl, z, 0, HALF), 5, 3, right)
    sib_send(rows(xl, z), rows(xl, z), 2)
    ag_wait(rows(xr, z), 5)
    ag_send(rows(xr, z, HALF, HALF), rows(xr, z, HALF, HALF), 6, 7, left)
    sib_send(rows(xr, z), rows(xr, z), 3)

    def base_of(px):
        return pl.multiple_of(px * GRP, GRP)

    def hidden_group(px, first, last):
        base = base_of(px)

        def body(i, carry):
            cols = pl.ds(pl.multiple_of(i * TILE, TILE), TILE)
            part = dot(na[:, pl.ds(base, GRP)], wg[pl.ds(base, GRP), cols], ((1,), (0,)))
            if not first:
                part = part + hacc[:, cols]
            if last:
                ostage[:, cols] = (aperm[:, cols].astype(F32) + part).astype(BF16)
            else:
                hacc[:, cols] = part
            return carry

        lax.fori_loop(0, C // TILE, body, 0)

    def grad_group(px):
        base = base_of(px)

        def body(i, carry):
            at = pl.multiple_of(base + i * 128, 128)
            gn[:, pl.ds(at, 128)] = dot(cperm[...], wg[pl.ds(at, 128)], ((1,), (1,)))
            return carry

        lax.fori_loop(0, GRP // 128, body, 0)

    sib_wait(x, z, 0)
    sib_wait(x, 1 - z, 1)
    hidden_group(x, True, False)
    grad_group(x)

    ag_wait(rows(xl, 1 - z), 2)
    ag_send(rows(xl, 1 - z, 0, HALF), rows(xl, 1 - z, 0, HALF), 7, 4, right)
    sib_send(rows(xl, 1 - z), rows(xl, 1 - z), 4)
    ag_wait(rows(xr, 1 - z), 6)
    ag_send(rows(xr, 1 - z, HALF, HALF), rows(xr, 1 - z, HALF, HALF), 8, 8, left)
    sib_send(rows(xr, 1 - z), rows(xr, 1 - z), 5)

    sib_wait(xl, z, 2)
    sib_wait(xl, 1 - z, 4)
    hidden_group(xl, False, False)
    grad_group(xl)
    sib_wait(xr, z, 3)
    sib_wait(xr, 1 - z, 5)
    hidden_group(xr, False, False)
    grad_group(xr)

    ag_wait(rows(x2, z, 0, HALF), 3)
    sib_send(rows(x2, z, 0, HALF), rows(x2, z, 0, HALF), 6)
    ag_wait(rows(x2, z, HALF, HALF), 7)
    sib_send(rows(x2, z, HALF, HALF), rows(x2, z, HALF, HALF), 7)
    ag_wait(rows(x2, 1 - z, 0, HALF), 4)
    sib_send(rows(x2, 1 - z, 0, HALF), rows(x2, 1 - z, 0, HALF), 8)
    ag_wait(rows(x2, 1 - z, HALF, HALF), 8)
    sib_send(rows(x2, 1 - z, HALF, HALF), rows(x2, 1 - z, HALF, HALF), 9)
    sib_wait(x2, z, 6, 0, HALF)
    sib_wait(x2, z, 7, HALF, HALF)
    sib_wait(x2, 1 - z, 8, 0, HALF)
    sib_wait(x2, 1 - z, 9, HALF, HALF)

    @pl.when(has_down)
    def _():
        pl.semaphore_signal(ready.at[0], inc=1, device_id=(down, q), device_id_type=MESH)

    @pl.when(has_up)
    def _():
        pl.semaphore_signal(ready.at[1], inc=1, device_id=(up, q), device_id_type=MESH)

    hidden_group(x2, False, True)

    def send_block(stage, out, k, section, p):
        remote(
            stage.at[pl.ds(pl.multiple_of(p * BLK, BLK), BLK)],
            out.at[pl.ds(pl.multiple_of(q * BLK, BLK), BLK)],
            a2a_ss.at[k], a2a_rs.at[k], (section, p),
        ).start()

    @pl.when(has_up)
    def _():
        def deal(i, carry):
            send_block(ostage, next_o, 0, up, lax.rem(q + START + STRIDE * i, PEERS))
            return carry

        pl.semaphore_wait(ready.at[0], 1)
        lax.fori_loop(0, PEERS, deal, 0)

    grad_group(x2)

    @pl.when(has_down)
    def _():
        pl.semaphore_wait(ready.at[1], 1)

    def grad_rows(i, carry):
        p = lax.rem(q + START + STRIDE * i, PEERS)
        r = pl.ds(pl.multiple_of(p * BLK, BLK), BLK)
        wide = bperm[r].astype(F32)
        rstd = lax.rsqrt(jnp.mean(wide * wide, axis=-1, keepdims=True) + EPS)
        scaled = gain[...] * gn[r]
        inner = jnp.mean(wide * scaled, axis=-1, keepdims=True)
        gstage[r] = (cperm[r].astype(F32) + rstd * scaled - wide * (rstd * rstd * rstd * inner)).astype(BF16)

        @pl.when(has_down)
        def _():
            send_block(gstage, back_o, 1, down, p)

        return carry

    lax.fori_loop(0, PEERS, grad_rows, 0)

    def slot(pz, pc):
        return cotq.at[pl.ds(pl.multiple_of(peer(0, pz, pc) * TOK, TOK), TOK)]

    def ex_wait(region, k):
        remote(region, region, ex_ss.at[0], ex_rs.at[k], sib).wait_recv()

    ex_wait(slot(1 - z, c), 1)
    send(slot(1 - z, c), slot(1 - z, c), ex_ss.at[2], ex_rs.at[2], sib)
    ex_wait(slot(z, 1 - c), 0)
    for k, src in enumerate((nb_sib, nb_z, nb_diag)):
        remote(nbq.at[src], nbq.at[src], nb_ss.at[0], nb_rs.at[k], sib).wait_recv()
    ex_wait(slot(1 - z, 1 - c), 2)

    def partial(px, cols):
        r = pl.ds(pl.multiple_of(px * SH, SH), SH)
        acc = dot(nbq[0, r], cotq[pl.ds(0, TOK), cols], ((1,), (0,)))
        for k in range(1, 4):
            acc = acc + dot(nbq[k, r], cotq[pl.ds(k * TOK, TOK), cols], ((1,), (0,)))
        return acc

    def partial_to(px, k):
        def body(i, carry):
            cols = pl.ds(pl.multiple_of(i * TILE, TILE), TILE)
            psend[k, :, cols] = partial(px, cols).astype(BF16)
            return carry

        lax.fori_loop(0, C // TILE, body, 0)

    first = pl.ds(0, HALF)
    second = pl.ds(HALF, HALF)
    partial_to(x2, 0)
    send(psend.at[0, first], rs_half.at[0], red_ss.at[0], red_rs.at[0], right)
    send(psend.at[0, second], rs_half.at[1], red_ss.at[1], red_rs.at[1], left)
    partial_to(xr, 1)
    send(psend.at[1, second], rs_full.at[0, second], red_ss.at[2], red_rs.at[3], right)
    partial_to(xl, 2)
    send(psend.at[2, first], rs_full.at[1, first], red_ss.at[3], red_rs.at[4], left)

    def own(i, carry):
        cols = pl.ds(pl.multiple_of(i * TILE, TILE), TILE)
        dw_o[:, cols] = partial(x, cols)
        return carry

    lax.fori_loop(0, C // TILE, own, 0)

    def add_half(k, half, region):
        def body(i, carry):
            r = pl.ds(pl.multiple_of(i * 16, 16), 16)
            at = pl.ds(pl.multiple_of(half * HALF + i * 16, 16), 16)
            psend[k, at] = (psend[k, at].astype(F32) + rs_half[half, r].astype(F32)).astype(BF16)
            return carry

        lax.fori_loop(0, HALF // 16, body, 0)

    remote(rs_half.at[0], rs_half.at[0], red_ss.at[0], red_rs.at[0], left).wait_recv()
    add_half(1, 0, first)
    send(psend.at[1, first], rs_full.at[0, first], red_ss.at[4], red_rs.at[2], right)
    remote(rs_half.at[1], rs_half.at[1], red_ss.at[0], red_rs.at[1], right).wait_recv()
    add_half(2, 1, second)
    send(psend.at[2, second], rs_full.at[1, second], red_ss.at[5], red_rs.at[5], left)

    for side in range(2):
        for h, part in enumerate((first, second)):
            region = rs_full.at[side, part]
            remote(region, region, red_ss.at[0], red_rs.at[2 + 2 * side + h], left).wait_recv()

    def finish(i, carry):
        r = pl.ds(pl.multiple_of(i * 16, 16), 16)
        dw_o[r] = (dw_o[r] + rs_full[0, r].astype(F32) + rs_full[1, r].astype(F32)) / count
        return carry

    lax.fori_loop(0, SH // 16, finish, 0)

    for cp in sent:
        cp.wait_send()

    @pl.when(has_up)
    def _():
        remote(ostage, next_o, a2a_ss.at[0], a2a_rs.at[0], sib).wait_send()

    @pl.when(has_down)
    def _():
        remote(gstage, back_o, a2a_ss.at[1], a2a_rs.at[1], sib).wait_send()

    @pl.when(has_down)
    def _():
        remote(ostage, next_o, a2a_ss.at[0], a2a_rs.at[0], sib).wait_recv()

    @pl.when(has_up)
    def _():
        remote(gstage, back_o, a2a_ss.at[1], a2a_rs.at[1], sib).wait_recv()


def local(acts_fwd, acts_bwd, cot_bwd, gain, proj, fwd_route, bwd_route, straggler):
    hbm = pl.BlockSpec(memory_space=pl.ANY)
    vmem = pl.BlockSpec(memory_space=pltpu.VMEM)
    smem = pl.BlockSpec(memory_space=pltpu.SMEM)
    dma = pltpu.SemaphoreType.DMA
    out = pl.pallas_call(
        kernel,
        name="swarm_tick",
        out_shape=(
            pltpu.VMEM((TOK, C), BF16),
            pltpu.VMEM((TOK, C), BF16),
            pltpu.VMEM((SH, C), F32),
        ),
        in_specs=[hbm, hbm, hbm, vmem, hbm, vmem, vmem, smem],
        out_specs=(vmem, vmem, vmem),
        scratch_shapes=[
            pltpu.VMEM((C, C), BF16),
            pltpu.VMEM((TOK, C), BF16),
            pltpu.VMEM((TOK, C), BF16),
            pltpu.VMEM((TOK, C), BF16),
            pltpu.VMEM((TOK, C), BF16),
            pltpu.VMEM((TOK, C), BF16),
            pltpu.VMEM((TOK, C), BF16),
            pltpu.VMEM((TOK, C), BF16),
            pltpu.VMEM((4, GRP, TOK), BF16),
            pltpu.VMEM((4, GRP, TOK), BF16),
            pltpu.VMEM((4 * TOK, C), BF16),
            pltpu.VMEM((TOK, C), F32),
            pltpu.VMEM((TOK, C), F32),
            pltpu.VMEM((TOK, C), BF16),
            pltpu.VMEM((TOK, C), BF16),
            pltpu.VMEM((3, SH, C), BF16),
            pltpu.VMEM((2, HALF, C), BF16),
            pltpu.VMEM((2, SH, C), BF16),
            dma((4,)),
            dma((9,)), dma((9,)),
            dma((10,)), dma((10,)),
            dma((3,)), dma((3,)),
            dma((3,)), dma((3,)),
            dma((6,)), dma((6,)),
            dma((2,)), dma((2,)),
            pltpu.SemaphoreType.REGULAR((2,)),
        ],
        compiler_params=pltpu.CompilerParams(
            collective_id=0, has_side_effects=True, vmem_limit_bytes=53 * 2**20
        ),
        cost_estimate=pl.CostEstimate(
            flops=6 * TOK * C * C, bytes_accessed=20 * 2**20, transcendentals=0
        ),
    )(
        acts_fwd[0], acts_bwd[0], cot_bwd[0], gain, proj[0],
        fwd_route.reshape(1, PEERS), bwd_route.reshape(1, PEERS), straggler,
    )
    return write_out(*out)


PARTS = 4


def write_kernel(a, b, w, ao, bo, wo, sem):
    moves = []
    for k in range(PARTS):
        for i, (src, dst) in enumerate(((a, ao.at[0]), (b, bo.at[0]), (w, wo.at[0]))):
            n = src.shape[0] // PARTS
            at = pl.ds(k * n, n)
            moves.append(pltpu.make_async_copy(src.at[at], dst.at[at], sem.at[k, i]))
    for move in moves:
        move.start()
    for move in moves:
        move.wait()


def write_out(*results):
    return pl.pallas_call(
        write_kernel,
        name="write_out",
        out_shape=tuple(jax.ShapeDtypeStruct((1, *v.shape), v.dtype) for v in results),
        in_specs=[pl.BlockSpec(memory_space=pltpu.VMEM)] * 3,
        out_specs=(pl.BlockSpec(memory_space=pl.ANY),) * 3,
        scratch_shapes=[pltpu.SemaphoreType.DMA((PARTS, 3))],
        compiler_params=pltpu.CompilerParams(vmem_limit_bytes=8 * 2**20),
    )(*results)


def solution(mesh):
    split = P("section", "peer", None)
    whole = P("section", None)
    return jax.shard_map(
        local,
        mesh=mesh,
        in_specs=(split, split, split, whole, split, split, split, whole),
        out_specs=(split, split, split),
        check_vma=False,
    )
```

```python
import jax
import jax.numpy as jnp
from jax import lax
from jax.experimental import pallas as pl
from jax.experimental.pallas import tpu as pltpu
from jax.sharding import PartitionSpec as P

MESH = pl.DeviceIdType.MESH
F32 = jnp.float32
BF16 = jnp.bfloat16
EPS = 1e-05
START = 7
STRIDE = 1

SECTIONS = 16
PEERS = 16
C = 2560
TOK = 256
BLK = 16
SH = C // PEERS
HALF = SH // 2
GRP = 4 * SH
TILE = 512


def dot(a, b, dims):
    return lax.dot_general(a, b, (dims, ((), ())), preferred_element_type=F32)


def kernel(
    acts_f, acts_b, cot, gain, proj, froute, broute, strag,
    next_o, back_o, dw_o,
    wg, af, ab, aperm, bperm, cperm, na, nb, nbt, nbq, cotq, hacc, gn, ostage, gstage,
    psend, rs_half, rs_full,
    loc_sem, ag_ss, ag_rs, sib_ss, sib_rs, ex_ss, ex_rs, nb_ss, nb_rs, red_ss, red_rs, a2a_ss, a2a_rs, ready, hello,
):
    s = lax.axis_index("section")
    q = lax.axis_index("peer")
    x = lax.div(q, 4)
    quad = lax.rem(q, 4)
    z = lax.div(quad, 2)
    c = lax.rem(q, 2)
    xr = lax.rem(x + 1, 4)
    xl = lax.rem(x + 3, 4)
    x2 = lax.rem(x + 2, 4)
    up = lax.rem(s + 1, SECTIONS)
    down = lax.rem(s + SECTIONS - 1, SECTIONS)

    def peer(px, pz, pc):
        return px * 4 + pz * 2 + pc

    right = (s, peer(xr, z, c))
    left = (s, peer(xl, z, c))
    zpart = (s, peer(x, 1 - z, c))
    sib = (s, peer(x, z, 1 - c))
    diag = (s, peer(x, 1 - z, 1 - c))

    bar = pltpu.get_barrier_semaphore()
    has_up = s < SECTIONS - 1
    has_down = s > 0
    for dev in (right, left, zpart, sib, diag):
        pl.semaphore_signal(bar, inc=1, device_id=dev, device_id_type=MESH)

    even = lax.rem(s, 2) == 0
    odd = lax.rem(s, 2) == 1

    @pl.when(even)
    def _():
        pl.semaphore_wait(bar, 5)

        @pl.when(has_up)
        def _():
            pl.semaphore_signal(bar, inc=1, device_id=(up, q), device_id_type=MESH)

        @pl.when(has_down)
        def _():
            pl.semaphore_signal(bar, inc=1, device_id=(down, q), device_id_type=MESH)

    @pl.when(odd)
    def _():
        pl.semaphore_wait(bar, 5 + has_up.astype(jnp.int32) + has_down.astype(jnp.int32))

        @pl.when(has_up)
        def _():
            pl.semaphore_signal(hello.at[1], inc=1, device_id=(up, q), device_id_type=MESH)

        @pl.when(has_down)
        def _():
            pl.semaphore_signal(hello.at[0], inc=1, device_id=(down, q), device_id_type=MESH)

    def remote(src, dst, ss, rs, dev):
        return pltpu.make_async_remote_copy(
            src_ref=src, dst_ref=dst, send_sem=ss, recv_sem=rs, device_id=dev, device_id_type=MESH
        )

    def rows(px, pz, lo=0, n=SH, pc=c):
        return wg.at[pl.ds(pl.multiple_of(peer(px, pz, pc) * SH + lo, 16), n)]

    sent = []

    def send(src, dst, ss, rs, dev):
        cp = remote(src, dst, ss, rs, dev)
        cp.start()
        sent.append(cp)

    def ag_send(src, region, k_send, k_recv, dev):
        send(src, region, ag_ss.at[k_send], ag_rs.at[k_recv], dev)

    def ag_wait(region, k_recv):
        remote(region, region, ag_ss.at[0], ag_rs.at[k_recv], zpart).wait_recv()

    def sib_send(src, region, k):
        send(src, region, sib_ss.at[k], sib_rs.at[k], sib)

    def sib_wait(px, pz, k, lo=0, n=SH):
        region = rows(px, pz, lo, n, 1 - c)
        remote(region, region, sib_ss.at[k], sib_rs.at[k], sib).wait_recv()

    ag_send(proj, rows(x, z), 0, 0, zpart)
    ag_send(proj, rows(x, z), 1, 1, right)
    ag_send(proj, rows(x, z), 2, 5, left)
    sib_send(proj, rows(x, z), 0)
    own_slot = pl.ds(pl.multiple_of(quad * TOK, TOK), TOK)
    loads = [
        pltpu.make_async_copy(acts_b, ab, loc_sem.at[0]),
        pltpu.make_async_copy(acts_f, af, loc_sem.at[1]),
        pltpu.make_async_copy(cot, cotq.at[own_slot], loc_sem.at[2]),
        pltpu.make_async_copy(proj, rows(x, z), loc_sem.at[3]),
    ]
    for cp in loads:
        cp.start()
    send(cot, cotq.at[own_slot], ex_ss.at[0], ex_rs.at[0], sib)

    count = jnp.float32(0)
    for i in range(PEERS):
        count = count + (1 - strag[0, i]).astype(F32)
    keep = (1 - strag[0, q]).astype(F32)

    loads[0].wait()

    def norm_b(i, carry):
        r = pl.ds(pl.multiple_of(i * 16, 16), 16)
        wide = ab[r].astype(F32)
        rstd = lax.rsqrt(jnp.mean(wide * wide, axis=-1, keepdims=True) + EPS)
        nb[r] = (wide * rstd * gain[...] * keep).astype(BF16)
        return carry

    lax.fori_loop(0, TOK // 16, norm_b, 0)

    def turn(i, carry):
        cols = pl.ds(pl.multiple_of(i * GRP, GRP), GRP)
        t = nb[:, cols].T
        for k in range(4):
            nbt[k, pl.ds(pl.multiple_of(i * SH, SH), SH)] = t[k * SH:(k + 1) * SH]
        return carry

    lax.fori_loop(0, 4, turn, 0)
    nb_sib = peer(0, z, 1 - c)
    nb_z = peer(0, 1 - z, c)
    nb_diag = peer(0, 1 - z, 1 - c)
    send(nbt.at[nb_sib], nbq.at[quad], nb_ss.at[0], nb_rs.at[0], sib)
    nbq[quad] = nbt[quad]

    def ordering(route_ref):
        st = (route_ref[...] == lax.broadcasted_iota(jnp.int32, (PEERS, PEERS), 0)).astype(F32).astype(BF16)
        e = ((lax.broadcasted_iota(jnp.int32, (TOK, PEERS), 0) >> 4)
             == lax.broadcasted_iota(jnp.int32, (TOK, PEERS), 1)).astype(F32).astype(BF16)
        er = dot(e, st, ((1,), (0,))).astype(BF16)
        full = dot(er, e, ((1,), (1,)))
        same = (lax.broadcasted_iota(jnp.int32, (TOK, TOK), 0) & 15) == (
            lax.broadcasted_iota(jnp.int32, (TOK, TOK), 1) & 15)
        return jnp.where(same, full, 0.0).astype(BF16)

    def reorder(order, src, dst):
        def body(i, carry):
            cols = pl.ds(pl.multiple_of(i * TILE, TILE), TILE)
            dst[:, cols] = dot(order, src[:, cols], ((1,), (0,))).astype(BF16)
            return carry

        lax.fori_loop(0, C // TILE, body, 0)

    loads[1].wait()
    reorder(ordering(froute), af, aperm)

    def norm_a(i, carry):
        r = pl.ds(pl.multiple_of(i * 16, 16), 16)
        wide = aperm[r].astype(F32)
        rstd = lax.rsqrt(jnp.mean(wide * wide, axis=-1, keepdims=True) + EPS)
        na[r] = (wide * rstd * gain[...]).astype(BF16)
        return carry

    lax.fori_loop(0, TOK // 16, norm_a, 0)
    order_b = ordering(broute)
    reorder(order_b, ab, bperm)
    loads[2].wait()
    reorder(order_b, cotq.at[own_slot], cperm)
    loads[3].wait()

    @pl.when(s == 0)
    def _():
        ostage[...] = jnp.zeros_like(ostage)
        zeros = pltpu.make_async_copy(ostage, next_o, loc_sem.at[0])
        zeros.start()
        zeros.wait()

    @pl.when(s == SECTIONS - 1)
    def _():
        gstage[...] = jnp.zeros_like(gstage)
        zeros = pltpu.make_async_copy(gstage, back_o, loc_sem.at[0])
        zeros.start()
        zeros.wait()

    ag_wait(rows(x, 1 - z), 0)
    ag_send(rows(x, 1 - z), rows(x, 1 - z), 3, 2, right)
    ag_send(rows(x, 1 - z), rows(x, 1 - z), 4, 6, left)
    sib_send(rows(x, 1 - z), rows(x, 1 - z), 1)
    send(cot, cotq.at[own_slot], ex_ss.at[1], ex_rs.at[1], zpart)
    send(nbt.at[nb_z], nbq.at[quad], nb_ss.at[1], nb_rs.at[1], zpart)
    send(nbt.at[nb_diag], nbq.at[quad], nb_ss.at[2], nb_rs.at[2], diag)

    ag_wait(rows(xl, z), 1)
    ag_send(rows(xl, z, 0, HALF), rows(xl, z, 0, HALF), 5, 3, right)
    sib_send(rows(xl, z), rows(xl, z), 2)
    ag_wait(rows(xr, z), 5)
    ag_send(rows(xr, z, HALF, HALF), rows(xr, z, HALF, HALF), 6, 7, left)
    sib_send(rows(xr, z), rows(xr, z), 3)

    def base_of(px):
        return pl.multiple_of(px * GRP, GRP)

    def hidden_group(px, first, last):
        base = base_of(px)

        def body(i, carry):
            cols = pl.ds(pl.multiple_of(i * TILE, TILE), TILE)
            part = dot(na[:, pl.ds(base, GRP)], wg[pl.ds(base, GRP), cols], ((1,), (0,)))
            if not first:
                part = part + hacc[:, cols]
            if last:
                ostage[:, cols] = (aperm[:, cols].astype(F32) + part).astype(BF16)
            else:
                hacc[:, cols] = part
            return carry

        lax.fori_loop(0, C // TILE, body, 0)

    def grad_group(px):
        base = base_of(px)

        def body(i, carry):
            at = pl.multiple_of(base + i * 128, 128)
            gn[:, pl.ds(at, 128)] = dot(cperm[...], wg[pl.ds(at, 128)], ((1,), (1,)))
            return carry

        lax.fori_loop(0, GRP // 128, body, 0)

    sib_wait(x, z, 0)
    sib_wait(x, 1 - z, 1)
    hidden_group(x, True, False)
    grad_group(x)

    ag_wait(rows(xl, 1 - z), 2)
    ag_send(rows(xl, 1 - z, 0, HALF), rows(xl, 1 - z, 0, HALF), 7, 4, right)
    sib_send(rows(xl, 1 - z), rows(xl, 1 - z), 4)
    ag_wait(rows(xr, 1 - z), 6)
    ag_send(rows(xr, 1 - z, HALF, HALF), rows(xr, 1 - z, HALF, HALF), 8, 8, left)
    sib_send(rows(xr, 1 - z), rows(xr, 1 - z), 5)

    sib_wait(xl, z, 2)
    sib_wait(xl, 1 - z, 4)
    hidden_group(xl, False, False)
    grad_group(xl)
    sib_wait(xr, z, 3)
    sib_wait(xr, 1 - z, 5)
    hidden_group(xr, False, False)
    grad_group(xr)

    ag_wait(rows(x2, z, 0, HALF), 3)
    sib_send(rows(x2, z, 0, HALF), rows(x2, z, 0, HALF), 6)
    ag_wait(rows(x2, z, HALF, HALF), 7)
    sib_send(rows(x2, z, HALF, HALF), rows(x2, z, HALF, HALF), 7)
    ag_wait(rows(x2, 1 - z, 0, HALF), 4)
    sib_send(rows(x2, 1 - z, 0, HALF), rows(x2, 1 - z, 0, HALF), 8)
    ag_wait(rows(x2, 1 - z, HALF, HALF), 8)
    sib_send(rows(x2, 1 - z, HALF, HALF), rows(x2, 1 - z, HALF, HALF), 9)
    sib_wait(x2, z, 6, 0, HALF)
    sib_wait(x2, z, 7, HALF, HALF)
    sib_wait(x2, 1 - z, 8, 0, HALF)
    sib_wait(x2, 1 - z, 9, HALF, HALF)

    @pl.when(even & has_up)
    def _():
        pl.semaphore_wait(hello.at[0], 1)

    @pl.when(even & has_down)
    def _():
        pl.semaphore_wait(hello.at[1], 1)

    @pl.when(has_down)
    def _():
        pl.semaphore_signal(ready.at[0], inc=1, device_id=(down, q), device_id_type=MESH)

    @pl.when(has_up)
    def _():
        pl.semaphore_signal(ready.at[1], inc=1, device_id=(up, q), device_id_type=MESH)

    hidden_group(x2, False, True)

    def offset_peer(i):
        j = lax.rem(i, 4)
        return lax.rem(q + 4 * (2 + 2 * j + lax.div(j, 2)) + lax.div(i, 4), PEERS)

    def send_block(stage, out, k, section, p):
        remote(
            stage.at[pl.ds(pl.multiple_of(p * BLK, BLK), BLK)],
            out.at[pl.ds(pl.multiple_of(q * BLK, BLK), BLK)],
            a2a_ss.at[k], a2a_rs.at[k], (section, p),
        ).start()

    @pl.when(has_up)
    def _():
        def deal(i, carry):
            send_block(ostage, next_o, 0, up, offset_peer(i))
            return carry

        pl.semaphore_wait(ready.at[0], 1)
        lax.fori_loop(0, PEERS, deal, 0)

    grad_group(x2)

    @pl.when(has_down)
    def _():
        pl.semaphore_wait(ready.at[1], 1)

    def grad_rows(i, carry):
        p = offset_peer(i)
        r = pl.ds(pl.multiple_of(p * BLK, BLK), BLK)
        wide = bperm[r].astype(F32)
        rstd = lax.rsqrt(jnp.mean(wide * wide, axis=-1, keepdims=True) + EPS)
        scaled = gain[...] * gn[r]
        inner = jnp.mean(wide * scaled, axis=-1, keepdims=True)
        gstage[r] = (cperm[r].astype(F32) + rstd * scaled - wide * (rstd * rstd * rstd * inner)).astype(BF16)

        @pl.when(has_down)
        def _():
            send_block(gstage, back_o, 1, down, p)

        return carry

    lax.fori_loop(0, PEERS, grad_rows, 0)

    def slot(pz, pc):
        return cotq.at[pl.ds(pl.multiple_of(peer(0, pz, pc) * TOK, TOK), TOK)]

    def ex_wait(region, k):
        remote(region, region, ex_ss.at[0], ex_rs.at[k], sib).wait_recv()

    ex_wait(slot(1 - z, c), 1)
    send(slot(1 - z, c), slot(1 - z, c), ex_ss.at[2], ex_rs.at[2], sib)
    ex_wait(slot(z, 1 - c), 0)
    for k, src in enumerate((nb_sib, nb_z, nb_diag)):
        remote(nbq.at[src], nbq.at[src], nb_ss.at[0], nb_rs.at[k], sib).wait_recv()
    ex_wait(slot(1 - z, 1 - c), 2)

    def partial(px, cols):
        r = pl.ds(pl.multiple_of(px * SH, SH), SH)
        acc = dot(nbq[0, r], cotq[pl.ds(0, TOK), cols], ((1,), (0,)))
        for k in range(1, 4):
            acc = acc + dot(nbq[k, r], cotq[pl.ds(k * TOK, TOK), cols], ((1,), (0,)))
        return acc

    def partial_to(px, k):
        def body(i, carry):
            cols = pl.ds(pl.multiple_of(i * TILE, TILE), TILE)
            psend[k, :, cols] = partial(px, cols).astype(BF16)
            return carry

        lax.fori_loop(0, C // TILE, body, 0)

    first = pl.ds(0, HALF)
    second = pl.ds(HALF, HALF)
    partial_to(x2, 0)
    send(psend.at[0, first], rs_half.at[0], red_ss.at[0], red_rs.at[0], right)
    send(psend.at[0, second], rs_half.at[1], red_ss.at[1], red_rs.at[1], left)
    partial_to(xr, 1)
    send(psend.at[1, second], rs_full.at[0, second], red_ss.at[2], red_rs.at[3], right)
    partial_to(xl, 2)
    send(psend.at[2, first], rs_full.at[1, first], red_ss.at[3], red_rs.at[4], left)

    def own(i, carry):
        cols = pl.ds(pl.multiple_of(i * TILE, TILE), TILE)
        dw_o[:, cols] = partial(x, cols)
        return carry

    lax.fori_loop(0, C // TILE, own, 0)

    def add_half(k, half, region):
        def body(i, carry):
            r = pl.ds(pl.multiple_of(i * 16, 16), 16)
            at = pl.ds(pl.multiple_of(half * HALF + i * 16, 16), 16)
            psend[k, at] = (psend[k, at].astype(F32) + rs_half[half, r].astype(F32)).astype(BF16)
            return carry

        lax.fori_loop(0, HALF // 16, body, 0)

    remote(rs_half.at[0], rs_half.at[0], red_ss.at[0], red_rs.at[0], left).wait_recv()
    add_half(1, 0, first)
    send(psend.at[1, first], rs_full.at[0, first], red_ss.at[4], red_rs.at[2], right)
    remote(rs_half.at[1], rs_half.at[1], red_ss.at[0], red_rs.at[1], right).wait_recv()
    add_half(2, 1, second)
    send(psend.at[2, second], rs_full.at[1, second], red_ss.at[5], red_rs.at[5], left)

    for side in range(2):
        for h, part in enumerate((first, second)):
            region = rs_full.at[side, part]
            remote(region, region, red_ss.at[0], red_rs.at[2 + 2 * side + h], left).wait_recv()

    def finish(i, carry):
        r = pl.ds(pl.multiple_of(i * 16, 16), 16)
        dw_o[r] = (dw_o[r] + rs_full[0, r].astype(F32) + rs_full[1, r].astype(F32)) / count
        return carry

    lax.fori_loop(0, SH // 16, finish, 0)

    for cp in sent:
        cp.wait_send()

    @pl.when(has_up)
    def _():
        remote(ostage, next_o, a2a_ss.at[0], a2a_rs.at[0], sib).wait_send()

    @pl.when(has_down)
    def _():
        remote(gstage, back_o, a2a_ss.at[1], a2a_rs.at[1], sib).wait_send()

    @pl.when(has_down)
    def _():
        remote(ostage, next_o, a2a_ss.at[0], a2a_rs.at[0], sib).wait_recv()

    @pl.when(has_up)
    def _():
        remote(gstage, back_o, a2a_ss.at[1], a2a_rs.at[1], sib).wait_recv()


def local(acts_fwd, acts_bwd, cot_bwd, gain, proj, fwd_route, bwd_route, straggler):
    hbm = pl.BlockSpec(memory_space=pl.ANY)
    vmem = pl.BlockSpec(memory_space=pltpu.VMEM)
    smem = pl.BlockSpec(memory_space=pltpu.SMEM)
    dma = pltpu.SemaphoreType.DMA
    out = pl.pallas_call(
        kernel,
        name="swarm_tick",
        out_shape=(
            pltpu.VMEM((TOK, C), BF16),
            pltpu.VMEM((TOK, C), BF16),
            pltpu.VMEM((SH, C), F32),
        ),
        in_specs=[hbm, hbm, hbm, vmem, hbm, vmem, vmem, smem],
        out_specs=(vmem, vmem, vmem),
        scratch_shapes=[
            pltpu.VMEM((C, C), BF16),
            pltpu.VMEM((TOK, C), BF16),
            pltpu.VMEM((TOK, C), BF16),
            pltpu.VMEM((TOK, C), BF16),
            pltpu.VMEM((TOK, C), BF16),
            pltpu.VMEM((TOK, C), BF16),
            pltpu.VMEM((TOK, C), BF16),
            pltpu.VMEM((TOK, C), BF16),
            pltpu.VMEM((4, GRP, TOK), BF16),
            pltpu.VMEM((4, GRP, TOK), BF16),
            pltpu.VMEM((4 * TOK, C), BF16),
            pltpu.VMEM((TOK, C), F32),
            pltpu.VMEM((TOK, C), F32),
            pltpu.VMEM((TOK, C), BF16),
            pltpu.VMEM((TOK, C), BF16),
            pltpu.VMEM((3, SH, C), BF16),
            pltpu.VMEM((2, HALF, C), BF16),
            pltpu.VMEM((2, SH, C), BF16),
            dma((4,)),
            dma((9,)), dma((9,)),
            dma((10,)), dma((10,)),
            dma((3,)), dma((3,)),
            dma((3,)), dma((3,)),
            dma((6,)), dma((6,)),
            dma((2,)), dma((2,)),
            pltpu.SemaphoreType.REGULAR((2,)),
            pltpu.SemaphoreType.REGULAR((2,)),
        ],
        compiler_params=pltpu.CompilerParams(
            collective_id=0, has_side_effects=True, vmem_limit_bytes=53 * 2**20
        ),
        cost_estimate=pl.CostEstimate(
            flops=6 * TOK * C * C, bytes_accessed=20 * 2**20, transcendentals=0
        ),
    )(
        acts_fwd[0], acts_bwd[0], cot_bwd[0], gain, proj[0],
        fwd_route.reshape(1, PEERS), bwd_route.reshape(1, PEERS), straggler,
    )
    return write_out(*out)


PARTS = 4


def write_kernel(a, b, w, ao, bo, wo, sem):
    moves = []
    for k in range(PARTS):
        for i, (src, dst) in enumerate(((a, ao.at[0]), (b, bo.at[0]), (w, wo.at[0]))):
            n = src.shape[0] // PARTS
            at = pl.ds(k * n, n)
            moves.append(pltpu.make_async_copy(src.at[at], dst.at[at], sem.at[k, i]))
    for move in moves:
        move.start()
    for move in moves:
        move.wait()


def write_out(*results):
    return pl.pallas_call(
        write_kernel,
        name="write_out",
        out_shape=tuple(jax.ShapeDtypeStruct((1, *v.shape), v.dtype) for v in results),
        in_specs=[pl.BlockSpec(memory_space=pltpu.VMEM)] * 3,
        out_specs=(pl.BlockSpec(memory_space=pl.ANY),) * 3,
        scratch_shapes=[pltpu.SemaphoreType.DMA((PARTS, 3))],
        compiler_params=pltpu.CompilerParams(vmem_limit_bytes=8 * 2**20),
    )(*results)


def solution(mesh):
    split = P("section", "peer", None)
    whole = P("section", None)
    return jax.shard_map(
        local,
        mesh=mesh,
        in_specs=(split, split, split, whole, split, split, split, whole),
        out_specs=(split, split, split),
        check_vma=False,
    )
```

```python
import jax
import jax.numpy as jnp
from jax import lax
from jax.experimental import pallas as pl
from jax.experimental.pallas import tpu as pltpu
from jax.sharding import PartitionSpec as P

MESH = pl.DeviceIdType.MESH
F32 = jnp.float32
BF16 = jnp.bfloat16
EPS = 1e-05
START = 7
STRIDE = 1

SECTIONS = 16
PEERS = 16
C = 2560
TOK = 256
BLK = 16
SH = C // PEERS
HALF = SH // 2
GRP = 4 * SH
TILE = 512


def dot(a, b, dims):
    return lax.dot_general(a, b, (dims, ((), ())), preferred_element_type=F32)


def kernel(
    acts_f, acts_b, cot, gain, proj, froute, broute, strag,
    next_o, back_o, dw_o,
    wg, af, ab, aperm, bperm, cperm, na, nb, nbt, nbq, cotq, hacc, gn, ostage, gstage,
    psend, rs_half, rs_full,
    loc_sem, ag_ss, ag_rs, sib_ss, sib_rs, ex_ss, ex_rs, nb_ss, nb_rs, red_ss, red_rs, a2a_ss, a2a_rs, ready, hello,
):
    s = lax.axis_index("section")
    q = lax.axis_index("peer")
    x = lax.div(q, 4)
    quad = lax.rem(q, 4)
    z = lax.div(quad, 2)
    c = lax.rem(q, 2)
    xr = lax.rem(x + 1, 4)
    xl = lax.rem(x + 3, 4)
    x2 = lax.rem(x + 2, 4)
    up = lax.rem(s + 1, SECTIONS)
    down = lax.rem(s + SECTIONS - 1, SECTIONS)

    def peer(px, pz, pc):
        return px * 4 + pz * 2 + pc

    right = (s, peer(xr, z, c))
    left = (s, peer(xl, z, c))
    zpart = (s, peer(x, 1 - z, c))
    sib = (s, peer(x, z, 1 - c))
    diag = (s, peer(x, 1 - z, 1 - c))

    bar = pltpu.get_barrier_semaphore()
    has_up = s < SECTIONS - 1
    has_down = s > 0
    for dev in (right, left, zpart, sib, diag):
        pl.semaphore_signal(bar, inc=1, device_id=dev, device_id_type=MESH)

    even = lax.rem(s, 2) == 0
    odd = lax.rem(s, 2) == 1

    @pl.when(even)
    def _():
        pl.semaphore_wait(bar, 5)

        @pl.when(has_up)
        def _():
            pl.semaphore_signal(bar, inc=1, device_id=(up, q), device_id_type=MESH)

        @pl.when(has_down)
        def _():
            pl.semaphore_signal(bar, inc=1, device_id=(down, q), device_id_type=MESH)

    @pl.when(odd)
    def _():
        pl.semaphore_wait(bar, 5 + has_up.astype(jnp.int32) + has_down.astype(jnp.int32))

        @pl.when(has_up)
        def _():
            pl.semaphore_signal(hello.at[1], inc=1, device_id=(up, q), device_id_type=MESH)

        @pl.when(has_down)
        def _():
            pl.semaphore_signal(hello.at[0], inc=1, device_id=(down, q), device_id_type=MESH)

    def remote(src, dst, ss, rs, dev):
        return pltpu.make_async_remote_copy(
            src_ref=src, dst_ref=dst, send_sem=ss, recv_sem=rs, device_id=dev, device_id_type=MESH
        )

    def rows(px, pz, lo=0, n=SH, pc=c):
        return wg.at[pl.ds(pl.multiple_of(peer(px, pz, pc) * SH + lo, 16), n)]

    sent = []

    def send(src, dst, ss, rs, dev):
        cp = remote(src, dst, ss, rs, dev)
        cp.start()
        sent.append(cp)

    def ag_send(src, region, k_send, k_recv, dev):
        send(src, region, ag_ss.at[k_send], ag_rs.at[k_recv], dev)

    def ag_wait(region, k_recv):
        remote(region, region, ag_ss.at[0], ag_rs.at[k_recv], zpart).wait_recv()

    def sib_send(src, region, k):
        send(src, region, sib_ss.at[k], sib_rs.at[k], sib)

    def sib_wait(px, pz, k, lo=0, n=SH):
        region = rows(px, pz, lo, n, 1 - c)
        remote(region, region, sib_ss.at[k], sib_rs.at[k], sib).wait_recv()

    ag_send(proj.at[pl.ds(0, HALF)], rows(x, z, 0, HALF), 0, 0, zpart)
    ag_send(proj.at[pl.ds(HALF, HALF)], rows(x, z, HALF, HALF), 9, 9, zpart)
    ag_send(proj, rows(x, z), 1, 1, right)
    ag_send(proj, rows(x, z), 2, 5, left)
    sib_send(proj, rows(x, z), 0)
    own_slot = pl.ds(pl.multiple_of(quad * TOK, TOK), TOK)
    loads = [
        pltpu.make_async_copy(acts_b, ab, loc_sem.at[0]),
        pltpu.make_async_copy(acts_f, af, loc_sem.at[1]),
        pltpu.make_async_copy(cot, cotq.at[own_slot], loc_sem.at[2]),
        pltpu.make_async_copy(proj, rows(x, z), loc_sem.at[3]),
    ]
    for cp in loads:
        cp.start()
    send(cot, cotq.at[own_slot], ex_ss.at[0], ex_rs.at[0], sib)

    count = jnp.float32(0)
    for i in range(PEERS):
        count = count + (1 - strag[0, i]).astype(F32)
    keep = (1 - strag[0, q]).astype(F32)

    loads[0].wait()

    def norm_b(i, carry):
        r = pl.ds(pl.multiple_of(i * 16, 16), 16)
        wide = ab[r].astype(F32)
        rstd = lax.rsqrt(jnp.mean(wide * wide, axis=-1, keepdims=True) + EPS)
        nb[r] = (wide * rstd * gain[...] * keep).astype(BF16)
        return carry

    lax.fori_loop(0, TOK // 16, norm_b, 0)

    def turn(i, carry):
        cols = pl.ds(pl.multiple_of(i * GRP, GRP), GRP)
        t = nb[:, cols].T
        for k in range(4):
            nbt[k, pl.ds(pl.multiple_of(i * SH, SH), SH)] = t[k * SH:(k + 1) * SH]
        return carry

    lax.fori_loop(0, 4, turn, 0)
    nb_sib = peer(0, z, 1 - c)
    nb_z = peer(0, 1 - z, c)
    nb_diag = peer(0, 1 - z, 1 - c)
    send(nbt.at[nb_sib], nbq.at[quad], nb_ss.at[0], nb_rs.at[0], sib)
    nbq[quad] = nbt[quad]

    def pass_on(half, k_recv, k_send, k_left, k_right):
        part = rows(x, 1 - z, half * HALF, HALF)
        ag_wait(part, k_recv)
        ag_send(part, part, k_send, k_left, right)
        ag_send(part, part, k_send + 1, k_right, left)

    pass_on(0, 0, 3, 2, 6)

    def ordering(route_ref):
        st = (route_ref[...] == lax.broadcasted_iota(jnp.int32, (PEERS, PEERS), 0)).astype(F32).astype(BF16)
        e = ((lax.broadcasted_iota(jnp.int32, (TOK, PEERS), 0) >> 4)
             == lax.broadcasted_iota(jnp.int32, (TOK, PEERS), 1)).astype(F32).astype(BF16)
        er = dot(e, st, ((1,), (0,))).astype(BF16)
        full = dot(er, e, ((1,), (1,)))
        same = (lax.broadcasted_iota(jnp.int32, (TOK, TOK), 0) & 15) == (
            lax.broadcasted_iota(jnp.int32, (TOK, TOK), 1) & 15)
        return jnp.where(same, full, 0.0).astype(BF16)

    def reorder(order, src, dst):
        def body(i, carry):
            cols = pl.ds(pl.multiple_of(i * TILE, TILE), TILE)
            dst[:, cols] = dot(order, src[:, cols], ((1,), (0,))).astype(BF16)
            return carry

        lax.fori_loop(0, C // TILE, body, 0)

    loads[1].wait()
    reorder(ordering(froute), af, aperm)

    def norm_a(i, carry):
        r = pl.ds(pl.multiple_of(i * 16, 16), 16)
        wide = aperm[r].astype(F32)
        rstd = lax.rsqrt(jnp.mean(wide * wide, axis=-1, keepdims=True) + EPS)
        na[r] = (wide * rstd * gain[...]).astype(BF16)
        return carry

    lax.fori_loop(0, TOK // 16, norm_a, 0)
    order_b = ordering(broute)
    reorder(order_b, ab, bperm)
    loads[2].wait()
    reorder(order_b, cotq.at[own_slot], cperm)
    loads[3].wait()

    @pl.when(s == 0)
    def _():
        ostage[...] = jnp.zeros_like(ostage)
        zeros = pltpu.make_async_copy(ostage, next_o, loc_sem.at[0])
        zeros.start()
        zeros.wait()

    @pl.when(s == SECTIONS - 1)
    def _():
        gstage[...] = jnp.zeros_like(gstage)
        zeros = pltpu.make_async_copy(gstage, back_o, loc_sem.at[0])
        zeros.start()
        zeros.wait()

    pass_on(1, 9, 10, 10, 11)
    sib_send(rows(x, 1 - z), rows(x, 1 - z), 1)
    send(cot, cotq.at[own_slot], ex_ss.at[1], ex_rs.at[1], zpart)
    send(nbt.at[nb_z], nbq.at[quad], nb_ss.at[1], nb_rs.at[1], zpart)
    send(nbt.at[nb_diag], nbq.at[quad], nb_ss.at[2], nb_rs.at[2], diag)

    ag_wait(rows(xl, z), 1)
    ag_send(rows(xl, z, 0, HALF), rows(xl, z, 0, HALF), 5, 3, right)
    sib_send(rows(xl, z), rows(xl, z), 2)
    ag_wait(rows(xr, z), 5)
    ag_send(rows(xr, z, HALF, HALF), rows(xr, z, HALF, HALF), 6, 7, left)
    sib_send(rows(xr, z), rows(xr, z), 3)

    def base_of(px):
        return pl.multiple_of(px * GRP, GRP)

    def hidden_group(px, first, last):
        base = base_of(px)

        def body(i, carry):
            cols = pl.ds(pl.multiple_of(i * TILE, TILE), TILE)
            part = dot(na[:, pl.ds(base, GRP)], wg[pl.ds(base, GRP), cols], ((1,), (0,)))
            if not first:
                part = part + hacc[:, cols]
            if last:
                ostage[:, cols] = (aperm[:, cols].astype(F32) + part).astype(BF16)
            else:
                hacc[:, cols] = part
            return carry

        lax.fori_loop(0, C // TILE, body, 0)

    def grad_group(px):
        base = base_of(px)

        def body(i, carry):
            at = pl.multiple_of(base + i * 128, 128)
            gn[:, pl.ds(at, 128)] = dot(cperm[...], wg[pl.ds(at, 128)], ((1,), (1,)))
            return carry

        lax.fori_loop(0, GRP // 128, body, 0)

    sib_wait(x, z, 0)
    sib_wait(x, 1 - z, 1)
    hidden_group(x, True, False)
    grad_group(x)

    ag_wait(rows(xl, 1 - z, 0, HALF), 2)
    ag_send(rows(xl, 1 - z, 0, HALF), rows(xl, 1 - z, 0, HALF), 7, 4, right)
    ag_wait(rows(xr, 1 - z, 0, HALF), 6)
    ag_wait(rows(xr, 1 - z, HALF, HALF), 11)
    ag_send(rows(xr, 1 - z, HALF, HALF), rows(xr, 1 - z, HALF, HALF), 8, 8, left)
    sib_send(rows(xr, 1 - z), rows(xr, 1 - z), 5)
    ag_wait(rows(xl, 1 - z, HALF, HALF), 10)
    sib_send(rows(xl, 1 - z), rows(xl, 1 - z), 4)

    sib_wait(xl, z, 2)
    sib_wait(xl, 1 - z, 4)
    hidden_group(xl, False, False)
    grad_group(xl)
    sib_wait(xr, z, 3)
    sib_wait(xr, 1 - z, 5)
    hidden_group(xr, False, False)
    grad_group(xr)

    ag_wait(rows(x2, z, 0, HALF), 3)
    sib_send(rows(x2, z, 0, HALF), rows(x2, z, 0, HALF), 6)
    ag_wait(rows(x2, z, HALF, HALF), 7)
    sib_send(rows(x2, z, HALF, HALF), rows(x2, z, HALF, HALF), 7)
    ag_wait(rows(x2, 1 - z, 0, HALF), 4)
    sib_send(rows(x2, 1 - z, 0, HALF), rows(x2, 1 - z, 0, HALF), 8)
    ag_wait(rows(x2, 1 - z, HALF, HALF), 8)
    sib_send(rows(x2, 1 - z, HALF, HALF), rows(x2, 1 - z, HALF, HALF), 9)
    sib_wait(x2, z, 6, 0, HALF)
    sib_wait(x2, z, 7, HALF, HALF)
    sib_wait(x2, 1 - z, 8, 0, HALF)
    sib_wait(x2, 1 - z, 9, HALF, HALF)

    @pl.when(even & has_up)
    def _():
        pl.semaphore_wait(hello.at[0], 1)

    @pl.when(even & has_down)
    def _():
        pl.semaphore_wait(hello.at[1], 1)

    @pl.when(has_down)
    def _():
        pl.semaphore_signal(ready.at[0], inc=1, device_id=(down, q), device_id_type=MESH)

    @pl.when(has_up)
    def _():
        pl.semaphore_signal(ready.at[1], inc=1, device_id=(up, q), device_id_type=MESH)

    hidden_group(x2, False, True)

    def offset_peer(i):
        j = lax.rem(i, 2)
        late = lax.div(i, 8)
        k = lax.rem(lax.div(i, 2), 4)
        return lax.rem(q + 4 * (2 + 2 * j + late) + k, PEERS)

    def send_block(stage, out, k, section, p):
        remote(
            stage.at[pl.ds(pl.multiple_of(p * BLK, BLK), BLK)],
            out.at[pl.ds(pl.multiple_of(q * BLK, BLK), BLK)],
            a2a_ss.at[k], a2a_rs.at[k], (section, p),
        ).start()

    @pl.when(has_up)
    def _():
        def deal(i, carry):
            send_block(ostage, next_o, 0, up, offset_peer(i))
            return carry

        pl.semaphore_wait(ready.at[0], 1)
        lax.fori_loop(0, PEERS, deal, 0)

    grad_group(x2)

    @pl.when(has_down)
    def _():
        pl.semaphore_wait(ready.at[1], 1)

    def grad_rows(i, carry):
        p = offset_peer(i)
        r = pl.ds(pl.multiple_of(p * BLK, BLK), BLK)
        wide = bperm[r].astype(F32)
        rstd = lax.rsqrt(jnp.mean(wide * wide, axis=-1, keepdims=True) + EPS)
        scaled = gain[...] * gn[r]
        inner = jnp.mean(wide * scaled, axis=-1, keepdims=True)
        gstage[r] = (cperm[r].astype(F32) + rstd * scaled - wide * (rstd * rstd * rstd * inner)).astype(BF16)

        @pl.when(has_down)
        def _():
            send_block(gstage, back_o, 1, down, p)

        return carry

    lax.fori_loop(0, PEERS, grad_rows, 0)

    def slot(pz, pc):
        return cotq.at[pl.ds(pl.multiple_of(peer(0, pz, pc) * TOK, TOK), TOK)]

    def ex_wait(region, k):
        remote(region, region, ex_ss.at[0], ex_rs.at[k], sib).wait_recv()

    ex_wait(slot(1 - z, c), 1)
    send(slot(1 - z, c), slot(1 - z, c), ex_ss.at[2], ex_rs.at[2], sib)
    ex_wait(slot(z, 1 - c), 0)
    for k, src in enumerate((nb_sib, nb_z, nb_diag)):
        remote(nbq.at[src], nbq.at[src], nb_ss.at[0], nb_rs.at[k], sib).wait_recv()
    ex_wait(slot(1 - z, 1 - c), 2)

    def partial(px, cols):
        r = pl.ds(pl.multiple_of(px * SH, SH), SH)
        acc = dot(nbq[0, r], cotq[pl.ds(0, TOK), cols], ((1,), (0,)))
        for k in range(1, 4):
            acc = acc + dot(nbq[k, r], cotq[pl.ds(k * TOK, TOK), cols], ((1,), (0,)))
        return acc

    def partial_to(px, k):
        def body(i, carry):
            cols = pl.ds(pl.multiple_of(i * TILE, TILE), TILE)
            psend[k, :, cols] = partial(px, cols).astype(BF16)
            return carry

        lax.fori_loop(0, C // TILE, body, 0)

    first = pl.ds(0, HALF)
    second = pl.ds(HALF, HALF)
    partial_to(x2, 0)
    send(psend.at[0, first], rs_half.at[0], red_ss.at[0], red_rs.at[0], right)
    send(psend.at[0, second], rs_half.at[1], red_ss.at[1], red_rs.at[1], left)
    partial_to(xr, 1)
    send(psend.at[1, second], rs_full.at[0, second], red_ss.at[2], red_rs.at[3], right)
    partial_to(xl, 2)
    send(psend.at[2, first], rs_full.at[1, first], red_ss.at[3], red_rs.at[4], left)

    def own(i, carry):
        cols = pl.ds(pl.multiple_of(i * TILE, TILE), TILE)
        dw_o[:, cols] = partial(x, cols)
        return carry

    lax.fori_loop(0, C // TILE, own, 0)

    def add_half(k, half, region):
        def body(i, carry):
            r = pl.ds(pl.multiple_of(i * 16, 16), 16)
            at = pl.ds(pl.multiple_of(half * HALF + i * 16, 16), 16)
            psend[k, at] = (psend[k, at].astype(F32) + rs_half[half, r].astype(F32)).astype(BF16)
            return carry

        lax.fori_loop(0, HALF // 16, body, 0)

    remote(rs_half.at[0], rs_half.at[0], red_ss.at[0], red_rs.at[0], left).wait_recv()
    add_half(1, 0, first)
    send(psend.at[1, first], rs_full.at[0, first], red_ss.at[4], red_rs.at[2], right)
    remote(rs_half.at[1], rs_half.at[1], red_ss.at[0], red_rs.at[1], right).wait_recv()
    add_half(2, 1, second)
    send(psend.at[2, second], rs_full.at[1, second], red_ss.at[5], red_rs.at[5], left)

    for side in range(2):
        for h, part in enumerate((first, second)):
            region = rs_full.at[side, part]
            remote(region, region, red_ss.at[0], red_rs.at[2 + 2 * side + h], left).wait_recv()

    def finish(i, carry):
        r = pl.ds(pl.multiple_of(i * 16, 16), 16)
        dw_o[r] = (dw_o[r] + rs_full[0, r].astype(F32) + rs_full[1, r].astype(F32)) / count
        return carry

    lax.fori_loop(0, SH // 16, finish, 0)

    for cp in sent:
        cp.wait_send()

    @pl.when(has_up)
    def _():
        remote(ostage, next_o, a2a_ss.at[0], a2a_rs.at[0], sib).wait_send()

    @pl.when(has_down)
    def _():
        remote(gstage, back_o, a2a_ss.at[1], a2a_rs.at[1], sib).wait_send()

    @pl.when(has_down)
    def _():
        remote(ostage, next_o, a2a_ss.at[0], a2a_rs.at[0], sib).wait_recv()

    @pl.when(has_up)
    def _():
        remote(gstage, back_o, a2a_ss.at[1], a2a_rs.at[1], sib).wait_recv()


def local(acts_fwd, acts_bwd, cot_bwd, gain, proj, fwd_route, bwd_route, straggler):
    hbm = pl.BlockSpec(memory_space=pl.ANY)
    vmem = pl.BlockSpec(memory_space=pltpu.VMEM)
    smem = pl.BlockSpec(memory_space=pltpu.SMEM)
    dma = pltpu.SemaphoreType.DMA
    out = pl.pallas_call(
        kernel,
        name="swarm_tick",
        out_shape=(
            pltpu.VMEM((TOK, C), BF16),
            pltpu.VMEM((TOK, C), BF16),
            pltpu.VMEM((SH, C), F32),
        ),
        in_specs=[hbm, hbm, hbm, vmem, hbm, vmem, vmem, smem],
        out_specs=(vmem, vmem, vmem),
        scratch_shapes=[
            pltpu.VMEM((C, C), BF16),
            pltpu.VMEM((TOK, C), BF16),
            pltpu.VMEM((TOK, C), BF16),
            pltpu.VMEM((TOK, C), BF16),
            pltpu.VMEM((TOK, C), BF16),
            pltpu.VMEM((TOK, C), BF16),
            pltpu.VMEM((TOK, C), BF16),
            pltpu.VMEM((TOK, C), BF16),
            pltpu.VMEM((4, GRP, TOK), BF16),
            pltpu.VMEM((4, GRP, TOK), BF16),
            pltpu.VMEM((4 * TOK, C), BF16),
            pltpu.VMEM((TOK, C), F32),
            pltpu.VMEM((TOK, C), F32),
            pltpu.VMEM((TOK, C), BF16),
            pltpu.VMEM((TOK, C), BF16),
            pltpu.VMEM((3, SH, C), BF16),
            pltpu.VMEM((2, HALF, C), BF16),
            pltpu.VMEM((2, SH, C), BF16),
            dma((4,)),
            dma((12,)), dma((12,)),
            dma((10,)), dma((10,)),
            dma((3,)), dma((3,)),
            dma((3,)), dma((3,)),
            dma((6,)), dma((6,)),
            dma((2,)), dma((2,)),
            pltpu.SemaphoreType.REGULAR((2,)),
            pltpu.SemaphoreType.REGULAR((2,)),
        ],
        compiler_params=pltpu.CompilerParams(
            collective_id=0, has_side_effects=True, vmem_limit_bytes=53 * 2**20
        ),
        cost_estimate=pl.CostEstimate(
            flops=6 * TOK * C * C, bytes_accessed=20 * 2**20, transcendentals=0
        ),
    )(
        acts_fwd[0], acts_bwd[0], cot_bwd[0], gain, proj[0],
        fwd_route.reshape(1, PEERS), bwd_route.reshape(1, PEERS), straggler,
    )
    return write_out(*out)


PARTS = 4


def write_kernel(a, b, w, ao, bo, wo, sem):
    moves = []
    for k in range(PARTS):
        for i, (src, dst) in enumerate(((a, ao.at[0]), (b, bo.at[0]), (w, wo.at[0]))):
            n = src.shape[0] // PARTS
            at = pl.ds(k * n, n)
            moves.append(pltpu.make_async_copy(src.at[at], dst.at[at], sem.at[k, i]))
    for move in moves:
        move.start()
    for move in moves:
        move.wait()


def write_out(*results):
    return pl.pallas_call(
        write_kernel,
        name="write_out",
        out_shape=tuple(jax.ShapeDtypeStruct((1, *v.shape), v.dtype) for v in results),
        in_specs=[pl.BlockSpec(memory_space=pltpu.VMEM)] * 3,
        out_specs=(pl.BlockSpec(memory_space=pl.ANY),) * 3,
        scratch_shapes=[pltpu.SemaphoreType.DMA((PARTS, 3))],
        compiler_params=pltpu.CompilerParams(vmem_limit_bytes=8 * 2**20),
    )(*results)


def solution(mesh):
    split = P("section", "peer", None)
    whole = P("section", None)
    return jax.shard_map(
        local,
        mesh=mesh,
        in_specs=(split, split, split, whole, split, split, split, whole),
        out_specs=(split, split, split),
        check_vma=False,
    )
```

```python
import jax
import jax.numpy as jnp
from jax import lax
from jax.experimental import pallas as pl
from jax.experimental.pallas import tpu as pltpu
from jax.sharding import PartitionSpec as P

MESH = pl.DeviceIdType.MESH
F32 = jnp.float32
BF16 = jnp.bfloat16
EPS = 1e-05
START = 7
STRIDE = 1

SECTIONS = 16
PEERS = 16
C = 2560
TOK = 256
BLK = 16
SH = C // PEERS
HALF = SH // 2
GRP = 4 * SH
TILE = 512


def dot(a, b, dims):
    return lax.dot_general(a, b, (dims, ((), ())), preferred_element_type=F32)


def kernel(
    acts_f, acts_b, cot, gain, proj, froute, broute, strag,
    next_o, back_o, dw_o,
    wg, af, ab, aperm, bperm, cperm, na, nb, nbt, nbq, cotq, hacc, gn, ostage, gstage,
    psend, rs_half, rs_full,
    loc_sem, ag_ss, ag_rs, sib_ss, sib_rs, ex_ss, ex_rs, nb_ss, nb_rs, red_ss, red_rs, a2a_ss, a2a_rs, ready, hello,
):
    s = lax.axis_index("section")
    q = lax.axis_index("peer")
    x = lax.div(q, 4)
    quad = lax.rem(q, 4)
    z = lax.div(quad, 2)
    c = lax.rem(q, 2)
    xr = lax.rem(x + 1, 4)
    xl = lax.rem(x + 3, 4)
    x2 = lax.rem(x + 2, 4)
    up = lax.rem(s + 1, SECTIONS)
    down = lax.rem(s + SECTIONS - 1, SECTIONS)

    def peer(px, pz, pc):
        return px * 4 + pz * 2 + pc

    right = (s, peer(xr, z, c))
    left = (s, peer(xl, z, c))
    zpart = (s, peer(x, 1 - z, c))
    sib = (s, peer(x, z, 1 - c))
    diag = (s, peer(x, 1 - z, 1 - c))

    bar = pltpu.get_barrier_semaphore()
    has_up = s < SECTIONS - 1
    has_down = s > 0
    for dev in (right, left, zpart, sib, diag):
        pl.semaphore_signal(bar, inc=1, device_id=dev, device_id_type=MESH)

    even = lax.rem(s, 2) == 0
    odd = lax.rem(s, 2) == 1

    @pl.when(even)
    def _():
        pl.semaphore_wait(bar, 5)

        @pl.when(has_up)
        def _():
            pl.semaphore_signal(bar, inc=1, device_id=(up, q), device_id_type=MESH)

        @pl.when(has_down)
        def _():
            pl.semaphore_signal(bar, inc=1, device_id=(down, q), device_id_type=MESH)

    @pl.when(odd)
    def _():
        pl.semaphore_wait(bar, 5 + has_up.astype(jnp.int32) + has_down.astype(jnp.int32))

        @pl.when(has_up)
        def _():
            pl.semaphore_signal(hello.at[1], inc=1, device_id=(up, q), device_id_type=MESH)

        @pl.when(has_down)
        def _():
            pl.semaphore_signal(hello.at[0], inc=1, device_id=(down, q), device_id_type=MESH)

    def remote(src, dst, ss, rs, dev):
        return pltpu.make_async_remote_copy(
            src_ref=src, dst_ref=dst, send_sem=ss, recv_sem=rs, device_id=dev, device_id_type=MESH
        )

    def rows(px, pz, lo=0, n=SH, pc=c):
        return wg.at[pl.ds(pl.multiple_of(peer(px, pz, pc) * SH + lo, 16), n)]

    sent = []

    def send(src, dst, ss, rs, dev):
        cp = remote(src, dst, ss, rs, dev)
        cp.start()
        sent.append(cp)

    def ag_send(src, region, k_send, k_recv, dev):
        send(src, region, ag_ss.at[k_send], ag_rs.at[k_recv], dev)

    def ag_wait(region, k_recv):
        remote(region, region, ag_ss.at[0], ag_rs.at[k_recv], zpart).wait_recv()

    def sib_send(src, region, k):
        send(src, region, sib_ss.at[k], sib_rs.at[k], sib)

    def sib_wait(px, pz, k, lo=0, n=SH):
        region = rows(px, pz, lo, n, 1 - c)
        remote(region, region, sib_ss.at[k], sib_rs.at[k], sib).wait_recv()

    ag_send(proj.at[pl.ds(0, HALF)], rows(x, z, 0, HALF), 0, 0, zpart)
    ag_send(proj.at[pl.ds(HALF, HALF)], rows(x, z, HALF, HALF), 9, 9, zpart)
    ag_send(proj, rows(x, z), 1, 1, right)
    ag_send(proj, rows(x, z), 2, 5, left)
    sib_send(proj, rows(x, z), 0)
    own_slot = pl.ds(pl.multiple_of(quad * TOK, TOK), TOK)
    loads = [
        pltpu.make_async_copy(acts_b, ab, loc_sem.at[0]),
        pltpu.make_async_copy(acts_f, af, loc_sem.at[1]),
        pltpu.make_async_copy(cot, cotq.at[own_slot], loc_sem.at[2]),
        pltpu.make_async_copy(proj, rows(x, z), loc_sem.at[3]),
    ]
    for cp in loads:
        cp.start()
    send(cot, cotq.at[own_slot], ex_ss.at[0], ex_rs.at[0], sib)

    count = jnp.float32(0)
    for i in range(PEERS):
        count = count + (1 - strag[0, i]).astype(F32)
    keep = (1 - strag[0, q]).astype(F32)

    loads[0].wait()

    def norm_b(i, carry):
        r = pl.ds(pl.multiple_of(i * 16, 16), 16)
        wide = ab[r].astype(F32)
        rstd = lax.rsqrt(jnp.mean(wide * wide, axis=-1, keepdims=True) + EPS)
        nb[r] = (wide * rstd * gain[...] * keep).astype(BF16)
        return carry

    lax.fori_loop(0, TOK // 16, norm_b, 0)

    def turn(i, carry):
        cols = pl.ds(pl.multiple_of(i * GRP, GRP), GRP)
        t = nb[:, cols].T
        for k in range(4):
            nbt[k, pl.ds(pl.multiple_of(i * SH, SH), SH)] = t[k * SH:(k + 1) * SH]
        return carry

    lax.fori_loop(0, 4, turn, 0)
    nb_sib = peer(0, z, 1 - c)
    nb_z = peer(0, 1 - z, c)
    nb_diag = peer(0, 1 - z, 1 - c)
    send(nbt.at[nb_sib], nbq.at[quad], nb_ss.at[0], nb_rs.at[0], sib)
    nbq[quad] = nbt[quad]

    def pass_on(half, k_recv, k_send, k_left, k_right):
        part = rows(x, 1 - z, half * HALF, HALF)
        ag_wait(part, k_recv)
        ag_send(part, part, k_send, k_left, right)
        ag_send(part, part, k_send + 1, k_right, left)

    pass_on(0, 0, 3, 2, 6)
    send(cot, cotq.at[own_slot], ex_ss.at[1], ex_rs.at[1], zpart)

    def ordering(route_ref):
        st = (route_ref[...] == lax.broadcasted_iota(jnp.int32, (PEERS, PEERS), 0)).astype(F32).astype(BF16)
        e = ((lax.broadcasted_iota(jnp.int32, (TOK, PEERS), 0) >> 4)
             == lax.broadcasted_iota(jnp.int32, (TOK, PEERS), 1)).astype(F32).astype(BF16)
        er = dot(e, st, ((1,), (0,))).astype(BF16)
        full = dot(er, e, ((1,), (1,)))
        same = (lax.broadcasted_iota(jnp.int32, (TOK, TOK), 0) & 15) == (
            lax.broadcasted_iota(jnp.int32, (TOK, TOK), 1) & 15)
        return jnp.where(same, full, 0.0).astype(BF16)

    def reorder(order, src, dst):
        def body(i, carry):
            cols = pl.ds(pl.multiple_of(i * TILE, TILE), TILE)
            dst[:, cols] = dot(order, src[:, cols], ((1,), (0,))).astype(BF16)
            return carry

        lax.fori_loop(0, C // TILE, body, 0)

    loads[1].wait()
    reorder(ordering(froute), af, aperm)

    def norm_a(i, carry):
        r = pl.ds(pl.multiple_of(i * 16, 16), 16)
        wide = aperm[r].astype(F32)
        rstd = lax.rsqrt(jnp.mean(wide * wide, axis=-1, keepdims=True) + EPS)
        na[r] = (wide * rstd * gain[...]).astype(BF16)
        return carry

    lax.fori_loop(0, TOK // 16, norm_a, 0)
    order_b = ordering(broute)
    reorder(order_b, ab, bperm)
    loads[2].wait()
    reorder(order_b, cotq.at[own_slot], cperm)
    loads[3].wait()

    @pl.when(s == 0)
    def _():
        ostage[...] = jnp.zeros_like(ostage)
        zeros = pltpu.make_async_copy(ostage, next_o, loc_sem.at[0])
        zeros.start()
        zeros.wait()

    @pl.when(s == SECTIONS - 1)
    def _():
        gstage[...] = jnp.zeros_like(gstage)
        zeros = pltpu.make_async_copy(gstage, back_o, loc_sem.at[0])
        zeros.start()
        zeros.wait()

    pass_on(1, 9, 10, 10, 11)
    sib_send(rows(x, 1 - z), rows(x, 1 - z), 1)
    send(nbt.at[nb_z], nbq.at[quad], nb_ss.at[1], nb_rs.at[1], zpart)
    send(nbt.at[nb_diag], nbq.at[quad], nb_ss.at[2], nb_rs.at[2], diag)

    ag_wait(rows(xl, z), 1)
    ag_send(rows(xl, z, 0, HALF), rows(xl, z, 0, HALF), 5, 3, right)
    sib_send(rows(xl, z), rows(xl, z), 2)
    ag_wait(rows(xr, z), 5)
    ag_send(rows(xr, z, HALF, HALF), rows(xr, z, HALF, HALF), 6, 7, left)
    sib_send(rows(xr, z), rows(xr, z), 3)

    def base_of(px):
        return pl.multiple_of(px * GRP, GRP)

    def hidden_group(px, first, last):
        base = base_of(px)

        def body(i, carry):
            cols = pl.ds(pl.multiple_of(i * TILE, TILE), TILE)
            part = dot(na[:, pl.ds(base, GRP)], wg[pl.ds(base, GRP), cols], ((1,), (0,)))
            if not first:
                part = part + hacc[:, cols]
            if last:
                ostage[:, cols] = (aperm[:, cols].astype(F32) + part).astype(BF16)
            else:
                hacc[:, cols] = part
            return carry

        lax.fori_loop(0, C // TILE, body, 0)

    def grad_group(px):
        base = base_of(px)

        def body(i, carry):
            at = pl.multiple_of(base + i * 128, 128)
            gn[:, pl.ds(at, 128)] = dot(cperm[...], wg[pl.ds(at, 128)], ((1,), (1,)))
            return carry

        lax.fori_loop(0, GRP // 128, body, 0)

    sib_wait(x, z, 0)
    sib_wait(x, 1 - z, 1)
    hidden_group(x, True, False)
    grad_group(x)

    ag_wait(rows(xl, 1 - z, 0, HALF), 2)
    ag_send(rows(xl, 1 - z, 0, HALF), rows(xl, 1 - z, 0, HALF), 7, 4, right)
    ag_wait(rows(xr, 1 - z, 0, HALF), 6)
    ag_wait(rows(xr, 1 - z, HALF, HALF), 11)
    ag_send(rows(xr, 1 - z, HALF, HALF), rows(xr, 1 - z, HALF, HALF), 8, 8, left)
    sib_send(rows(xr, 1 - z), rows(xr, 1 - z), 5)
    ag_wait(rows(xl, 1 - z, HALF, HALF), 10)
    sib_send(rows(xl, 1 - z), rows(xl, 1 - z), 4)

    sib_wait(xl, z, 2)
    sib_wait(xl, 1 - z, 4)
    hidden_group(xl, False, False)
    grad_group(xl)
    sib_wait(xr, z, 3)
    sib_wait(xr, 1 - z, 5)
    hidden_group(xr, False, False)
    grad_group(xr)

    ag_wait(rows(x2, z, 0, HALF), 3)
    sib_send(rows(x2, z, 0, HALF), rows(x2, z, 0, HALF), 6)
    ag_wait(rows(x2, z, HALF, HALF), 7)
    sib_send(rows(x2, z, HALF, HALF), rows(x2, z, HALF, HALF), 7)
    ag_wait(rows(x2, 1 - z, 0, HALF), 4)
    sib_send(rows(x2, 1 - z, 0, HALF), rows(x2, 1 - z, 0, HALF), 8)
    ag_wait(rows(x2, 1 - z, HALF, HALF), 8)
    sib_send(rows(x2, 1 - z, HALF, HALF), rows(x2, 1 - z, HALF, HALF), 9)
    sib_wait(x2, z, 6, 0, HALF)
    sib_wait(x2, z, 7, HALF, HALF)
    sib_wait(x2, 1 - z, 8, 0, HALF)
    sib_wait(x2, 1 - z, 9, HALF, HALF)

    @pl.when(even & has_up)
    def _():
        pl.semaphore_wait(hello.at[0], 1)

    @pl.when(even & has_down)
    def _():
        pl.semaphore_wait(hello.at[1], 1)

    @pl.when(has_down)
    def _():
        pl.semaphore_signal(ready.at[0], inc=1, device_id=(down, q), device_id_type=MESH)

    @pl.when(has_up)
    def _():
        pl.semaphore_signal(ready.at[1], inc=1, device_id=(up, q), device_id_type=MESH)

    hidden_group(x2, False, True)

    def offset_peer(i):
        j = lax.rem(i, 2)
        late = lax.div(i, 8)
        k = lax.rem(lax.div(i, 2), 4)
        return lax.rem(q + 4 * (2 + 2 * j + late) + k, PEERS)

    def send_block(stage, out, k, section, p):
        remote(
            stage.at[pl.ds(pl.multiple_of(p * BLK, BLK), BLK)],
            out.at[pl.ds(pl.multiple_of(q * BLK, BLK), BLK)],
            a2a_ss.at[k], a2a_rs.at[k], (section, p),
        ).start()

    @pl.when(has_up)
    def _():
        def deal(i, carry):
            send_block(ostage, next_o, 0, up, offset_peer(i))
            return carry

        pl.semaphore_wait(ready.at[0], 1)
        lax.fori_loop(0, PEERS, deal, 0)

    grad_group(x2)

    @pl.when(has_down)
    def _():
        pl.semaphore_wait(ready.at[1], 1)

    def grad_rows(i, carry):
        p = offset_peer(i)
        r = pl.ds(pl.multiple_of(p * BLK, BLK), BLK)
        wide = bperm[r].astype(F32)
        rstd = lax.rsqrt(jnp.mean(wide * wide, axis=-1, keepdims=True) + EPS)
        scaled = gain[...] * gn[r]
        inner = jnp.mean(wide * scaled, axis=-1, keepdims=True)
        gstage[r] = (cperm[r].astype(F32) + rstd * scaled - wide * (rstd * rstd * rstd * inner)).astype(BF16)

        @pl.when(has_down)
        def _():
            send_block(gstage, back_o, 1, down, p)

        return carry

    lax.fori_loop(0, PEERS, grad_rows, 0)

    def slot(pz, pc):
        return cotq.at[pl.ds(pl.multiple_of(peer(0, pz, pc) * TOK, TOK), TOK)]

    def ex_wait(region, k):
        remote(region, region, ex_ss.at[0], ex_rs.at[k], sib).wait_recv()

    ex_wait(slot(1 - z, c), 1)
    send(slot(1 - z, c), slot(1 - z, c), ex_ss.at[2], ex_rs.at[2], sib)
    ex_wait(slot(z, 1 - c), 0)
    for k, src in enumerate((nb_sib, nb_z, nb_diag)):
        remote(nbq.at[src], nbq.at[src], nb_ss.at[0], nb_rs.at[k], sib).wait_recv()
    ex_wait(slot(1 - z, 1 - c), 2)

    def partial(px, cols):
        r = pl.ds(pl.multiple_of(px * SH, SH), SH)
        acc = dot(nbq[0, r], cotq[pl.ds(0, TOK), cols], ((1,), (0,)))
        for k in range(1, 4):
            acc = acc + dot(nbq[k, r], cotq[pl.ds(k * TOK, TOK), cols], ((1,), (0,)))
        return acc

    def partial_to(px, k):
        def body(i, carry):
            cols = pl.ds(pl.multiple_of(i * TILE, TILE), TILE)
            psend[k, :, cols] = partial(px, cols).astype(BF16)
            return carry

        lax.fori_loop(0, C // TILE, body, 0)

    first = pl.ds(0, HALF)
    second = pl.ds(HALF, HALF)
    partial_to(x2, 0)
    send(psend.at[0, first], rs_half.at[0], red_ss.at[0], red_rs.at[0], right)
    send(psend.at[0, second], rs_half.at[1], red_ss.at[1], red_rs.at[1], left)
    partial_to(xr, 1)
    send(psend.at[1, second], rs_full.at[0, second], red_ss.at[2], red_rs.at[3], right)
    partial_to(xl, 2)
    send(psend.at[2, first], rs_full.at[1, first], red_ss.at[3], red_rs.at[4], left)

    def own(i, carry):
        cols = pl.ds(pl.multiple_of(i * TILE, TILE), TILE)
        dw_o[:, cols] = partial(x, cols)
        return carry

    lax.fori_loop(0, C // TILE, own, 0)

    def add_half(k, half, region):
        def body(i, carry):
            r = pl.ds(pl.multiple_of(i * 16, 16), 16)
            at = pl.ds(pl.multiple_of(half * HALF + i * 16, 16), 16)
            psend[k, at] = (psend[k, at].astype(F32) + rs_half[half, r].astype(F32)).astype(BF16)
            return carry

        lax.fori_loop(0, HALF // 16, body, 0)

    remote(rs_half.at[0], rs_half.at[0], red_ss.at[0], red_rs.at[0], left).wait_recv()
    add_half(1, 0, first)
    send(psend.at[1, first], rs_full.at[0, first], red_ss.at[4], red_rs.at[2], right)
    remote(rs_half.at[1], rs_half.at[1], red_ss.at[0], red_rs.at[1], right).wait_recv()
    add_half(2, 1, second)
    send(psend.at[2, second], rs_full.at[1, second], red_ss.at[5], red_rs.at[5], left)

    for side in range(2):
        for h, part in enumerate((first, second)):
            region = rs_full.at[side, part]
            remote(region, region, red_ss.at[0], red_rs.at[2 + 2 * side + h], left).wait_recv()

    def finish(i, carry):
        r = pl.ds(pl.multiple_of(i * 16, 16), 16)
        dw_o[r] = (dw_o[r] + rs_full[0, r].astype(F32) + rs_full[1, r].astype(F32)) / count
        return carry

    lax.fori_loop(0, SH // 16, finish, 0)

    for cp in sent:
        cp.wait_send()

    @pl.when(has_up)
    def _():
        remote(ostage, next_o, a2a_ss.at[0], a2a_rs.at[0], sib).wait_send()

    @pl.when(has_down)
    def _():
        remote(gstage, back_o, a2a_ss.at[1], a2a_rs.at[1], sib).wait_send()

    @pl.when(has_down)
    def _():
        remote(ostage, next_o, a2a_ss.at[0], a2a_rs.at[0], sib).wait_recv()

    @pl.when(has_up)
    def _():
        remote(gstage, back_o, a2a_ss.at[1], a2a_rs.at[1], sib).wait_recv()


def local(acts_fwd, acts_bwd, cot_bwd, gain, proj, fwd_route, bwd_route, straggler):
    hbm = pl.BlockSpec(memory_space=pl.ANY)
    vmem = pl.BlockSpec(memory_space=pltpu.VMEM)
    smem = pl.BlockSpec(memory_space=pltpu.SMEM)
    dma = pltpu.SemaphoreType.DMA
    out = pl.pallas_call(
        kernel,
        name="swarm_tick",
        out_shape=(
            pltpu.VMEM((TOK, C), BF16),
            pltpu.VMEM((TOK, C), BF16),
            pltpu.VMEM((SH, C), F32),
        ),
        in_specs=[hbm, hbm, hbm, vmem, hbm, vmem, vmem, smem],
        out_specs=(vmem, vmem, vmem),
        scratch_shapes=[
            pltpu.VMEM((C, C), BF16),
            pltpu.VMEM((TOK, C), BF16),
            pltpu.VMEM((TOK, C), BF16),
            pltpu.VMEM((TOK, C), BF16),
            pltpu.VMEM((TOK, C), BF16),
            pltpu.VMEM((TOK, C), BF16),
            pltpu.VMEM((TOK, C), BF16),
            pltpu.VMEM((TOK, C), BF16),
            pltpu.VMEM((4, GRP, TOK), BF16),
            pltpu.VMEM((4, GRP, TOK), BF16),
            pltpu.VMEM((4 * TOK, C), BF16),
            pltpu.VMEM((TOK, C), F32),
            pltpu.VMEM((TOK, C), F32),
            pltpu.VMEM((TOK, C), BF16),
            pltpu.VMEM((TOK, C), BF16),
            pltpu.VMEM((3, SH, C), BF16),
            pltpu.VMEM((2, HALF, C), BF16),
            pltpu.VMEM((2, SH, C), BF16),
            dma((4,)),
            dma((12,)), dma((12,)),
            dma((10,)), dma((10,)),
            dma((3,)), dma((3,)),
            dma((3,)), dma((3,)),
            dma((6,)), dma((6,)),
            dma((2,)), dma((2,)),
            pltpu.SemaphoreType.REGULAR((2,)),
            pltpu.SemaphoreType.REGULAR((2,)),
        ],
        compiler_params=pltpu.CompilerParams(
            collective_id=0, has_side_effects=True, vmem_limit_bytes=53 * 2**20
        ),
        cost_estimate=pl.CostEstimate(
            flops=6 * TOK * C * C, bytes_accessed=20 * 2**20, transcendentals=0
        ),
    )(
        acts_fwd[0], acts_bwd[0], cot_bwd[0], gain, proj[0],
        fwd_route.reshape(1, PEERS), bwd_route.reshape(1, PEERS), straggler,
    )
    return write_out(*out)


PARTS = 4


def write_kernel(a, b, w, ao, bo, wo, sem):
    moves = []
    for k in range(PARTS):
        for i, (src, dst) in enumerate(((a, ao.at[0]), (b, bo.at[0]), (w, wo.at[0]))):
            n = src.shape[0] // PARTS
            at = pl.ds(k * n, n)
            moves.append(pltpu.make_async_copy(src.at[at], dst.at[at], sem.at[k, i]))
    for move in moves:
        move.start()
    for move in moves:
        move.wait()


def write_out(*results):
    return pl.pallas_call(
        write_kernel,
        name="write_out",
        out_shape=tuple(jax.ShapeDtypeStruct((1, *v.shape), v.dtype) for v in results),
        in_specs=[pl.BlockSpec(memory_space=pltpu.VMEM)] * 3,
        out_specs=(pl.BlockSpec(memory_space=pl.ANY),) * 3,
        scratch_shapes=[pltpu.SemaphoreType.DMA((PARTS, 3))],
        compiler_params=pltpu.CompilerParams(vmem_limit_bytes=8 * 2**20),
    )(*results)


def solution(mesh):
    split = P("section", "peer", None)
    whole = P("section", None)
    return jax.shard_map(
        local,
        mesh=mesh,
        in_specs=(split, split, split, whole, split, split, split, whole),
        out_specs=(split, split, split),
        check_vma=False,
    )
```
